128 devices in a mesh: wide: 16 (over x, y), narrow: 8 (over z, core).
Axes of the slice: x: 4, y: 4, z: 4, core: 2. Of those that a mesh axis runs over, the one named last changes fastest.
Arguments:
- incident: bfloat16 [2, 4, 6, 262144], P(None, None, None, ('wide', 'narrow')), may hold values from -6 to 6
- jitter: bfloat16 [2, 262144], P(None, ('wide', 'narrow')), may hold values from -0.079589844 to 0.079589844
- weights: float32 [262144], P(('wide', 'narrow')), may hold values from 0.3 to 3
- cells: int32 [262144], P(('wide', 'narrow')), may hold values from 0 to 8191
- pair_list: int32 [128, 8, 3], P(('wide', 'narrow')), may hold values from 0 to 15, as said below
- pair_count: int32 [128], P(('wide', 'narrow')), may hold values from 1 to 8, as said below
- kernel: float32 [2, 1024, 1024], P(None, None, ('wide', 'narrow')), may hold values from -6 to 6
Outputs:
- coupled: float32 [2, 4, 6, 262144], P(None, None, None, ('wide', 'narrow'))
The draws below stay inside these ranges and needn't reach their ends.
Inputs may be any that keep to these rules, and one draw needn't show every extreme that they name: `pair_list`: each row names a direction t, an own cluster and a partner cluster, both below 16; the partner device exists on the tile grid, and for t = 0 the two clusters differ. The partner cluster b lies on the partner's side facing the own device: b % 4 == 0 for t = 1, b < 4 for t = 2, b = 3 for t = 3, b = 15 for t = 4. All slots hold such rows. `pair_count`: some device uses all 8 slots. Pillar p of device d lies in grid row d * 8 + cells[p] // 1024 and column cells[p] % 1024.
All inputs are finite; a program needn't handle non-finite values.
Results may differ from the reference program's by a relative error of at most 0.0025.
Values may be sent and summed in bfloat16 or wider, within the bound.
No kernel may reach another device: no remote copies, remote signals or barrier semaphores. Data moves between devices by JAX's collectives and lax.ppermute only.
A program may use at most 128 MiB of HBM per device.

```python
import math
import jax
import jax.numpy as jnp
import numpy as np
from jax import lax

ANG = 4
PCX = 8
PCY = 16
CCX = 4
CCY = 4
PAIRS = 8
CBX = 8
GY = 1024
PIL = 128
CL_DEV = 16
PIL_DEV = 2048
NPIL = 262144
GX = 1024
N_WIDE = 16
N_NARROW = 8
DEVICES = 128


def draw_pair_list(key, part):
    key = jax.random.fold_in(key, 11)
    keys = jax.random.split(key, 7)
    device = jnp.arange(DEVICES, dtype=jnp.int32)[:, None]
    wide_pos = device // N_NARROW
    narrow_pos = device % N_NARROW
    picked = jax.random.randint(keys[0], (DEVICES, PAIRS), 0, 5, dtype=jnp.int32)
    okay_one = narrow_pos + 1 < N_NARROW
    okay_two = wide_pos + 1 < N_WIDE
    okay_three = okay_two & (narrow_pos >= 1)
    okay_four = (wide_pos >= 1) & (narrow_pos >= 1)
    allowed = jnp.select([picked == 1, picked == 2, picked == 3, picked == 4], [okay_one, okay_two, okay_three, okay_four], True)
    direction = jnp.where(allowed, picked, 0)
    own_row = jax.random.randint(keys[1], (DEVICES, PAIRS), 0, CCX, dtype=jnp.int32)
    own_col = jax.random.randint(keys[2], (DEVICES, PAIRS), 0, CCY, dtype=jnp.int32)
    far_row = jax.random.randint(keys[3], (DEVICES, PAIRS), 0, CCX, dtype=jnp.int32)
    far_col = jax.random.randint(keys[4], (DEVICES, PAIRS), 0, CCY, dtype=jnp.int32)
    same_own = jax.random.randint(keys[5], (DEVICES, PAIRS), 0, CL_DEV, dtype=jnp.int32)
    same_far = (same_own + 1 + jax.random.randint(keys[6], (DEVICES, PAIRS), 0, CL_DEV - 1, dtype=jnp.int32)) % CL_DEV
    own_cluster = jnp.select([direction == 0, direction == 1, direction == 2, direction == 3], [same_own, own_row * CCY + (CCY - 1), (CCX - 1) * CCY + own_col, (CCX - 1) * CCY + 0 * own_col], 0 * own_col)
    far_cluster = jnp.select([direction == 0, direction == 1, direction == 2, direction == 3], [same_far, far_row * CCY, far_col, CCY - 1 + 0 * far_col], (CCX - 1) * CCY + (CCY - 1) + 0 * far_col)
    return jnp.stack([direction, own_cluster, far_cluster], axis=-1).astype(jnp.int32)


def draw_pair_count(key, part):
    key = jax.random.fold_in(key, 12)
    first, second = jax.random.split(key)
    counts = jax.random.randint(first, (DEVICES,), 1, PAIRS + 1, dtype=jnp.int32)
    busiest = jax.random.randint(second, (), 0, DEVICES, dtype=jnp.int32)
    return jnp.where(jnp.arange(DEVICES, dtype=jnp.int32) == busiest, PAIRS, counts).astype(jnp.int32)


def set_ends(values, own_key, smallest, high):
    index_at = [jax.random.randint(jax.random.fold_in(own_key, axis), (), 0, length) for axis, length in enumerate(values.shape)]
    longest = values.shape.index(max(values.shape))
    next_to = index_at[:longest] + [(index_at[longest] + 1) % values.shape[longest]] + index_at[longest + 1:]
    return values.at[tuple(index_at)].set(smallest).at[tuple(next_to)].set(high)


def shard_levels(key, extent, cuts, smallest, high):
    factor_of, own = 1.0, jax.random.fold_in(key, 6)
    for position, shards_of in cuts:
        heights = jnp.exp(jax.random.uniform(jax.random.fold_in(own, position), (shards_of,), jnp.float32, smallest / len(cuts), high / len(cuts)))
        factor_of = factor_of * jnp.repeat(heights, extent[position] // shards_of).reshape([-1 if axis == position else 1 for axis in range(len(extent))])
    return factor_of


def normal_values(rng, shape, scale, most, cuts=(), kind=jnp.bfloat16):
    drawn = jax.random.normal(rng, shape, jnp.float32) * scale
    if len(cuts) > 0:
        drawn = shard_levels(rng, shape, cuts, -0.22, 0.18) * drawn
    return jnp.clip(drawn, min=-most, max=most).astype(kind)


def setup_inputs(seed: int = 0) -> dict:
    arg_keys = jax.random.split(jax.random.key(seed), 8)
    return {
        "incident": normal_values(arg_keys[0], (2, ANG, 6, NPIL), 1.0, 6.0, ((3, 128),)),
        "jitter": jnp.clip(jax.random.uniform(arg_keys[1], (2, NPIL), jnp.float32, -0.079589844, 0.079589844) * shard_levels(arg_keys[1], (2, NPIL), ((1, 128),), -0.4, 0.0), -0.079589844, 0.079589844).astype(jnp.bfloat16),
        "weights": jnp.clip(jnp.exp(math.log(3.0) - 2.3025851 * jax.random.uniform(arg_keys[2], (NPIL,), jnp.float32) ** shard_levels(arg_keys[2], (NPIL,), ((0, 128),), -0.2, 0.2)), 0.3, 3.0),
        "cells": set_ends(jax.random.randint(arg_keys[3], (NPIL,), 0, CBX * GY), jax.random.fold_in(arg_keys[3], 1), 0, (CBX * GY) - 1).astype(jnp.int32),
        "pair_list": draw_pair_list(jax.random.fold_in(arg_keys[7], 71), 0),
        "pair_count": draw_pair_count(jax.random.fold_in(arg_keys[7], 71), 0),
        "kernel": normal_values(arg_keys[6], (2, GX, GY), 1.0, 6.0, ((2, 128),), jnp.float32),
    }


WAVE = 2.0 * math.pi
PITCH = 0.4
STEP_WIDE = (0, 0, 1, 1, -1)
STEP_NARROW = (0, 1, 0, -1, -1)

def coupling_table():
    table = np.zeros((6, 6, 6), np.float32)
    for member in range(6):
        table[0, member, member] = 1.0
    for offset in (0, 3):
        table[1, offset, offset] = 1.0
        table[2, offset, offset + 1] = 1.0
        table[2, offset + 1, offset] = 1.0
        table[3, offset + 1, offset + 1] = 1.0
    table[4, 2, 4] = 1.0
    table[4, 4, 2] = 1.0
    table[4, 1, 5] = -1.0
    table[4, 5, 1] = -1.0
    table[5, 0, 5] = 1.0
    table[5, 5, 0] = 1.0
    table[5, 2, 3] = -1.0
    table[5, 3, 2] = -1.0
    return table

def lattice(wide_pos, narrow_pos, cluster, offsets):
    local_ids = jnp.arange(PIL, dtype=jnp.int32)
    across = ((wide_pos * CCX + cluster // CCY) * PCX + local_ids // PCY).astype(jnp.float32)
    along = ((narrow_pos * CCY + cluster % CCY) * PCY + local_ids % PCY).astype(jnp.float32)
    return (across * PITCH + offsets[0], along * PITCH + offsets[1])

def near_fields(delta_x, delta_y):
    distance = jnp.sqrt(delta_x * delta_x + delta_y * delta_y)
    phase = WAVE * distance
    inverse = 1.0 / phase
    unit_x = delta_x / distance
    unit_y = delta_y / distance
    green_re = jnp.cos(phase) * inverse
    green_im = jnp.sin(phase) * inverse

    def times_green(first, second):
        return (green_re * first - green_im * second, green_re * second + green_im * first)
    term_a = times_green(1.0 - inverse * inverse, inverse)
    term_b = times_green(3.0 * inverse * inverse - 1.0, -3.0 * inverse)
    term_c = times_green(jnp.ones_like(inverse), inverse)

    def stacked(part):
        return jnp.stack([term_a[part], term_b[part] * unit_x * unit_x, term_b[part] * unit_x * unit_y, term_b[part] * unit_y * unit_y, term_c[part] * unit_x, term_c[part] * unit_y])
    return (stacked(0).astype(jnp.bfloat16), stacked(1).astype(jnp.bfloat16))

def mix_parts(prod_re, prod_im):
    shaped_re = prod_re.reshape(6, 2, ANG, 6, -1)
    shaped_im = prod_im.reshape(6, 2, ANG, 6, -1)
    real_part = shaped_re[:, 0] - shaped_im[:, 1]
    imag_part = shaped_re[:, 1] + shaped_im[:, 0]
    return jnp.stack([real_part, imag_part], 1)

def couple(field_re, field_im, left, right):
    coupling = jnp.asarray(coupling_table(), dtype=jnp.float32)
    high = lax.Precision.HIGHEST
    wide_re = field_re.astype(jnp.float32)
    wide_im = field_im.astype(jnp.float32)
    forward = mix_parts(jnp.einsum('fpq,cq->fcp', wide_re, right, precision=high), jnp.einsum('fpq,cq->fcp', wide_im, right, precision=high))
    to_left = jnp.einsum('fab,frgbp->rgap', coupling, forward, precision=high).reshape(-1, PIL)
    backward = mix_parts(jnp.einsum('fpq,cp->fcq', wide_re, left, precision=high), jnp.einsum('fpq,cp->fcq', wide_im, left, precision=high))
    to_right = jnp.einsum('fab,frgaq->rgbq', coupling, backward, precision=high).reshape(-1, PIL)
    return (to_left, to_right)

def reference(incident, jitter, weights, cells, pair_list, pair_count, kernel):
    channels = 12 * ANG
    half_chan = 6 * ANG
    fields = incident.reshape(channels, NPIL).astype(jnp.float32)
    offsets = jitter.astype(jnp.float32)
    step_wide = jnp.array(STEP_WIDE, dtype=jnp.int32)
    step_narrow = jnp.array(STEP_NARROW, dtype=jnp.int32)

    def one_device(device):
        wide_pos = device // N_NARROW
        narrow_pos = device % N_NARROW

        def one_pair(slot_idx):
            pair_row = pair_list[device, slot_idx]
            direction = pair_row[0]
            own_cluster = pair_row[1]
            far_cluster = pair_row[2]
            partner_wide = wide_pos + step_wide[direction]
            partner_narrow = narrow_pos + step_narrow[direction]
            partner = partner_wide * N_NARROW + partner_narrow
            own_start = ((device * CL_DEV + own_cluster) * PIL).astype(jnp.int32)
            far_start = ((partner * CL_DEV + far_cluster) * PIL).astype(jnp.int32)
            own_vals = lax.dynamic_slice_in_dim(fields, own_start, PIL, 1)
            far_vals = lax.dynamic_slice_in_dim(fields, far_start, PIL, 1)
            own_x, own_y = lattice(wide_pos, narrow_pos, own_cluster, lax.dynamic_slice_in_dim(offsets, own_start, PIL, 1))
            far_x, far_y = lattice(partner_wide, partner_narrow, far_cluster, lax.dynamic_slice_in_dim(offsets, far_start, PIL, 1))
            field_re, field_im = near_fields(own_x[:, None] - far_x[None, :], own_y[:, None] - far_y[None, :])
            to_left, to_right = couple(field_re, field_im, own_vals, far_vals)
            active = (slot_idx < pair_count[device]).astype(jnp.float32)
            return (to_left * active, to_right * active, own_start, far_start)
        return jax.vmap(one_pair)(jnp.arange(PAIRS, dtype=jnp.int32))
    to_left, to_right, own_starts, far_starts = lax.map(one_device, jnp.arange(DEVICES, dtype=jnp.int32))

    def spread(values, starts):
        columns = (starts[..., None] + jnp.arange(PIL, dtype=jnp.int32)).reshape(-1)
        data = jnp.moveaxis(values, 2, 0).reshape(channels, -1)
        return (columns, data)
    near_sum = jnp.zeros((channels, NPIL), dtype=jnp.float32)
    columns, data = spread(to_left, own_starts)
    near_sum = near_sum.at[:, columns].add(data)
    columns, data = spread(to_right, far_starts)
    near_sum = near_sum.at[:, columns].add(data)
    pillar_ids = jnp.arange(NPIL, dtype=jnp.int32)
    flat_cell = pillar_ids // PIL_DEV * (CBX * GY) + cells
    scaled = fields * weights[None, :]
    grid = jax.ops.segment_sum(scaled.T, flat_cell, num_segments=GX * GY).reshape(GX, GY, channels)
    complex_grid = lax.complex(grid[..., :half_chan], grid[..., half_chan:])
    spectrum = jnp.fft.fft2(complex_grid, axes=(0, 1))
    transfer = lax.complex(kernel[0], kernel[1])[:, :, None]
    far_grid = jnp.fft.ifft2(spectrum * transfer, axes=(0, 1))
    far_real = jnp.concatenate([jnp.real(far_grid), jnp.imag(far_grid)], axis=2).reshape(GX * GY, channels)
    sampled = jnp.take(far_real, flat_cell, axis=0).T * weights[None, :]
    return (near_sum + sampled).reshape(2, ANG, 6, NPIL)
```

```python
import math

import jax
import jax.numpy as jnp
import numpy as np
from jax import lax
from jax.experimental import pallas as pl
from jax.experimental.pallas import tpu as pltpu
from jax.sharding import PartitionSpec as P

ANG = 4
PCX = 8
PCY = 16
CCX = 4
CCY = 4
PIL = 128
CHAN = 48
HALF = 24
WIDTH = 2048
PAIRS = 8
N_WIDE = 16
N_NARROW = 8
DEVICES = 128
AXES = ("wide", "narrow")
PITCH = 0.4
BF16 = jnp.bfloat16
F32 = jnp.float32
HALO = 10
MIB = 1 << 20


def split_table(table):
    high = table.astype(BF16)
    low = (table - high.astype(np.float64)).astype(BF16)
    return np.stack([high, low])


def dft_table(sign, scale=1.0):
    ids = np.arange(128)
    angles = (ids[:, None] * ids[None, :] % 128) * (2.0 * math.pi / 128)
    cosine = np.cos(angles) * scale
    sine = np.sin(angles) * scale * sign
    return split_table(np.block([[cosine, -sine], [sine, cosine]]))


def row_twiddle():
    k1 = np.repeat(np.arange(8), 8)
    angles = (k1[:, None] * np.arange(128)[None, :]) * (2.0 * math.pi / 1024)
    return np.stack([np.cos(angles), -np.sin(angles)]).astype(np.float32)


def column_twiddle():
    row = (np.arange(128) // 64)[None, None, :] + 2 * np.arange(4)[:, None, None]
    angles = (row * np.arange(128)[None, :, None]) * (2.0 * math.pi / 1024)
    return np.stack([np.cos(angles), -np.sin(angles)]).reshape(2, 512, 128).astype(np.float32)


def lane_twiddle():
    side = (np.arange(128) // 64)[None, :]
    angles = np.arange(4)[:, None] * side * (2.0 * math.pi / 8)
    table = np.concatenate([np.cos(angles), -np.sin(angles), np.where(side == 0, 1.0, -1.0)])
    return np.concatenate([table, np.zeros((7, 128))]).astype(np.float32)


def mixing_table():
    table = np.zeros((6, 6, 6), np.float32)
    for member in range(6):
        table[0, member, member] = 1.0
    for offset in (0, 3):
        table[1, offset, offset] = 1.0
        table[2, offset, offset + 1] = 1.0
        table[2, offset + 1, offset] = 1.0
        table[3, offset + 1, offset + 1] = 1.0
    table[4, 2, 4] = 1.0
    table[4, 4, 2] = 1.0
    table[4, 1, 5] = -1.0
    table[4, 5, 1] = -1.0
    table[5, 0, 5] = 1.0
    table[5, 5, 0] = 1.0
    table[5, 2, 3] = -1.0
    table[5, 3, 2] = -1.0
    parts = np.zeros((2, 2, 2), np.float32)
    parts[0] = np.eye(2)
    parts[1] = np.array([[0.0, -1.0], [1.0, 0.0]])
    full = np.einsum("fab,rop,gh->frogapb" + "h", table, parts, np.eye(ANG))
    full = full.transpose(0, 1, 2, 3, 4, 5, 7, 6)
    return full.reshape(12 * CHAN, CHAN).astype(BF16)


def dot(left, right, left_dim=1, right_dim=0):
    return lax.dot_general(
        left, right, (((left_dim,), (right_dim,)), ((), ())), preferred_element_type=F32
    )


def halves(value):
    high = value.astype(BF16)
    return high, (value - high.astype(F32)).astype(BF16)


def cadd(left, right):
    return (left[0] + right[0], left[1] + right[1])


def csub(left, right):
    return (left[0] - right[0], left[1] - right[1])


def cmul(left, right):
    return (left[0] * right[0] - left[1] * right[1], left[0] * right[1] + left[1] * right[0])


def cmul_conj(left, right):
    return (left[0] * right[0] + left[1] * right[1], left[1] * right[0] - left[0] * right[1])


def turn(value, sign):
    if sign < 0:
        return (value[1], -value[0])
    return (-value[1], value[0])


def dft4(values, sign):
    even, odd = cadd(values[0], values[2]), csub(values[0], values[2])
    left, right = cadd(values[1], values[3]), turn(csub(values[1], values[3]), sign)
    return [cadd(even, left), cadd(odd, right), csub(even, left), csub(odd, right)]


def dft8(values, sign):
    even = dft4(values[0::2], sign)
    odd = dft4(values[1::2], sign)
    root = math.sqrt(0.5)
    first, third = odd[1], odd[3]
    odd[1] = ((first[0] - sign * first[1]) * root, (first[1] + sign * first[0]) * root)
    odd[2] = turn(odd[2], sign)
    odd[3] = ((-third[0] - sign * third[1]) * root, (-third[1] + sign * third[0]) * root)
    return [cadd(e, o) for e, o in zip(even, odd)] + [csub(e, o) for e, o in zip(even, odd)]


def rows_kernel(x_ref, w_ref, cell_ref, dft_ref, tw_ref, out_ref, xt_ref, hot_ref, g_ref, b_ref):
    cells = cell_ref[...]
    upper = cells >> 8
    weight = w_ref[...]
    high = weight.astype(BF16).astype(F32)
    low = weight - high
    for block in range(16):
        place = lax.broadcasted_iota(jnp.int32, (16, WIDTH), 0) + block * 16
        hit = place == (cells & 255)
        hot_ref[0, block * 16 : block * 16 + 16, :] = jnp.where(hit, high, 0.0).astype(BF16)
        hot_ref[1, block * 16 : block * 16 + 16, :] = jnp.where(hit, low, 0.0).astype(BF16)
    for part in range(32):
        mask = jnp.where(upper == part, 1.0, 0.0).astype(BF16)
        xt_ref[part * CHAN : (part + 1) * CHAN, :] = x_ref[...] * mask
    for chunk in range(2):
        rows = slice(chunk * 768, (chunk + 1) * 768)
        piece = xt_ref[rows, :]
        g_ref[rows, :] = dot(piece, hot_ref[0], 1, 1) + dot(piece, hot_ref[1], 1, 1)

    def one_row(row, carry):
        for t in range(3):
            values = []
            for n1 in range(8):
                start = (row * 4 + n1 // 2) * CHAN + t * 8
                lanes = slice((n1 % 2) * 128, (n1 % 2) * 128 + 128)
                values.append(
                    (
                        g_ref[pl.ds(pl.multiple_of(start, 8), 8), lanes],
                        g_ref[pl.ds(pl.multiple_of(start + HALF, 8), 8), lanes],
                    )
                )
            values = dft8(values, -1.0)
            base = (((row // 2) * 3 + t) * 2 + row % 2) * 64
            for k1 in range(8):
                value = values[k1]
                if k1 > 0:
                    twiddle = (
                        tw_ref[0, k1 * 8 : k1 * 8 + 8, :],
                        tw_ref[1, k1 * 8 : k1 * 8 + 8, :],
                    )
                    value = cmul(value, twiddle)
                rows = pl.ds(pl.multiple_of(base + k1 * 8, 8), 8)
                b_ref[rows, 0:128] = value[0]
                b_ref[rows, 128:256] = value[1]
        return carry

    lax.fori_loop(0, 8, one_row, 0)
    for pair in range(6):
        b_high, b_low = halves(b_ref[pair * 256 : (pair + 1) * 256, :])
        result = (
            dot(dft_ref[0], b_high, 1, 1) + dot(dft_ref[0], b_low, 1, 1) + dot(dft_ref[1], b_high, 1, 1)
        )
        for part in range(2):
            for side in range(2):
                out_ref[pl.ds(part * 12 + pair * 2 + side, 128, 24), :] = result[
                    part * 128 : (part + 1) * 128, side * 128 : (side + 1) * 128
                ]


def columns_kernel(r_ref, kern_ref, fwd_ref, inv_ref, tw_ref, lane_ref, out_ref, v_ref, u_ref):
    for part in range(2):
        for group in range(12):
            v_ref[part * 128 : (part + 1) * 128, group * 128 : (group + 1) * 128] = r_ref[
                pl.ds(part * 12 + group, 128, 24), :
            ]
    for chunk in range(6):
        lanes = slice(chunk * 256, (chunk + 1) * 256)
        v_high, v_low = halves(v_ref[:, lanes])
        u_ref[:, lanes] = dot(fwd_ref[0], v_high) + dot(fwd_ref[0], v_low) + dot(fwd_ref[1], v_high)
    sign = lane_ref[8:9, :]

    def swap(value):
        return tuple(part * sign + pltpu.roll(part, 64, 1) for part in value)

    def one_block(block, carry):
        start = pl.multiple_of(block * 8, 8)
        re_rows = pl.ds(start, 8)
        im_rows = pl.ds(pl.multiple_of(start + 128, 8), 8)
        twiddles, kernels = [], []
        for m in range(4):
            rows = pl.ds(pl.multiple_of(start + m * 128, 8), 8)
            twiddles.append((tw_ref[0, rows, :], tw_ref[1, rows, :]))
            kernels.append((kern_ref[0, rows, :], kern_ref[1, rows, :]))
        for t in range(3):
            values = []
            for m in range(4):
                lanes = slice((m * 3 + t) * 128, (m * 3 + t + 1) * 128)
                values.append(cmul((u_ref[re_rows, lanes], u_ref[im_rows, lanes]), twiddles[m]))
            values = dft4(values, -1.0)
            for a in range(4):
                side = (lane_ref[a : a + 1, :], lane_ref[4 + a : 5 + a, :])
                value = values[a] if a == 0 else cmul(values[a], side)
                value = swap(cmul(swap(value), kernels[a]))
                values[a] = value if a == 0 else cmul_conj(value, side)
            values = dft4(values, 1.0)
            for m in range(4):
                lanes = slice((m * 3 + t) * 128, (m * 3 + t + 1) * 128)
                value = cmul_conj(values[m], twiddles[m])
                v_ref[re_rows, lanes] = value[0]
                v_ref[im_rows, lanes] = value[1]
        return carry

    lax.fori_loop(0, 16, one_block, 0)
    for chunk in range(6):
        lanes = slice(chunk * 256, (chunk + 1) * 256)
        v_high, v_low = halves(v_ref[:, lanes])
        result = dot(inv_ref[0], v_high) + dot(inv_ref[0], v_low) + dot(inv_ref[1], v_high)
        for part in range(2):
            for side in range(2):
                out_ref[pl.ds(part * 12 + chunk * 2 + side, 128, 24), :] = result[
                    part * 128 : (part + 1) * 128, side * 128 : (side + 1) * 128
                ]


def sample_kernel(
    r_ref, w_ref, cell_ref, near_ref, one_ref, two_ref, three_ref, four_ref, dft_ref, tw_ref,
    out_ref, v_ref, g_ref, f_ref,
):
    for part in range(2):
        for group in range(12):
            piece = r_ref[pl.ds(part * 12 + group, 128, 24), :]
            v_ref[group * 128 : (group + 1) * 128, part * 128 : (part + 1) * 128] = piece.T
    for chunk in range(2):
        rows = slice(chunk * 768, (chunk + 1) * 768)
        v_high, v_low = halves(v_ref[rows, :])
        g_ref[rows, :] = (
            dot(v_high, dft_ref[0], 1, 1) + dot(v_low, dft_ref[0], 1, 1) + dot(v_high, dft_ref[1], 1, 1)
        )

    def one_row(row, carry):
        for t in range(3):
            base = (((row // 2) * 3 + t) * 2 + row % 2) * 64
            values = []
            for k1 in range(8):
                rows = pl.ds(pl.multiple_of(base + k1 * 8, 8), 8)
                value = (g_ref[rows, 0:128], g_ref[rows, 128:256])
                if k1 > 0:
                    twiddle = (
                        tw_ref[0, k1 * 8 : k1 * 8 + 8, :],
                        tw_ref[1, k1 * 8 : k1 * 8 + 8, :],
                    )
                    value = cmul_conj(value, twiddle)
                values.append(value)
            values = dft8(values, 1.0)
            for n1 in range(8):
                start = (row * 4 + n1 // 2) * CHAN + t * 8
                lanes = slice((n1 % 2) * 128, (n1 % 2) * 128 + 128)
                v_ref[pl.ds(pl.multiple_of(start, 8), 8), lanes] = values[n1][0]
                v_ref[pl.ds(pl.multiple_of(start + HALF, 8), 8), lanes] = values[n1][1]
        return carry

    lax.fori_loop(0, 8, one_row, 0)
    f_high, f_low = halves(v_ref[...])
    f_ref[0] = f_high
    f_ref[1] = f_low
    place = lax.broadcasted_iota(jnp.int32, (256, 256), 0)
    for chunk in range(8):
        lanes = slice(chunk * 256, (chunk + 1) * 256)
        cells = cell_ref[:, lanes]
        hot = jnp.where(place == (cells & 255), 1.0, 0.0).astype(BF16)
        upper = cells >> 8
        total = jnp.zeros((CHAN, 256), F32)
        for quarter in range(4):
            rows = slice(quarter * 384, (quarter + 1) * 384)
            picked = dot(f_ref[0, rows, :], hot) + dot(f_ref[1, rows, :], hot)
            for part in range(8):
                hit = jnp.broadcast_to(upper == quarter * 8 + part, (CHAN, 256))
                total = total + jnp.where(hit, picked[part * CHAN : (part + 1) * CHAN, :], 0.0)
        out_ref[:, lanes] = total * w_ref[:, lanes] + near_ref[:, lanes]
    for cluster in range(4):
        lanes = slice(cluster * 4 * PIL, (cluster * 4 + 1) * PIL)
        out_ref[:, lanes] += one_ref[:, cluster * PIL : (cluster + 1) * PIL].astype(F32)
        lanes = slice(cluster * PIL, (cluster + 1) * PIL)
        out_ref[:, lanes] += two_ref[:, cluster * PIL : (cluster + 1) * PIL].astype(F32)
    out_ref[:, 3 * PIL : 4 * PIL] += three_ref[...].astype(F32)
    out_ref[:, 15 * PIL : 16 * PIL] += four_ref[...].astype(F32)


def taylor(count, first):
    return [(-1.0) ** n / math.factorial(2 * n + first) for n in range(count)]


def horner(coefficients, square):
    total = jnp.full_like(square, coefficients[-1])
    for coefficient in coefficients[-2::-1]:
        total = total * square + coefficient
    return total


def near_kernel(
    list_ref, own_ref, one_ref, two_ref, three_ref, four_ref, own_pos, one_pos, two_pos, three_pos,
    four_pos, mix_ref, near_ref, back_one, back_two, back_three, back_four, all_ref, pos_ref, sum_ref,
):
    all_ref[:, 0:WIDTH] = own_ref[...]
    pos_ref[0:2, 0:WIDTH] = own_pos[...].astype(F32)
    start = WIDTH
    for data, pos in ((one_ref, one_pos), (two_ref, two_pos), (three_ref, three_pos), (four_ref, four_pos)):
        width = data.shape[1]
        all_ref[:, start : start + width] = data[...]
        pos_ref[0:2, start : start + width] = pos[...].astype(F32)
        start += width
    sum_ref[...] = jnp.zeros_like(sum_ref)
    wide_pos = list_ref[24]
    narrow_pos = list_ref[25]
    used = list_ref[26]
    local = lax.broadcasted_iota(jnp.int32, (1, PIL), 1)

    def place(wide, narrow, cluster, window):
        across = ((wide * CCX + cluster // CCY) * PCX + local // PCY).astype(F32)
        along = ((narrow * CCY + cluster % CCY) * PCY + local % PCY).astype(F32)
        return across * PITCH + pos_ref[0:1, window], along * PITCH + pos_ref[1:2, window]

    def column(vector):
        return jnp.broadcast_to(vector, (PIL, PIL)).T

    def mixed(values):
        return dot(mix_ref[...], values).astype(BF16)

    def one_slot(slot, carry):
        direction = list_ref[slot * 3]
        own = list_ref[slot * 3 + 1]
        far = list_ref[slot * 3 + 2]
        move_wide = jnp.where(direction == 4, -1, jnp.where(direction >= 2, 1, 0))
        move_narrow = jnp.where(direction == 1, 1, jnp.where(direction >= 3, -1, 0))
        index = jnp.where(direction == 1, 16 + far // 4, far)
        index = jnp.where(direction == 2, 20 + far, index)
        index = jnp.where(direction == 3, 24, index)
        index = jnp.where(direction == 4, 25, index)
        own_window = pl.ds(pl.multiple_of(own * PIL, PIL), PIL)
        far_window = pl.ds(pl.multiple_of(index * PIL, PIL), PIL)
        own_x, own_y = place(wide_pos, narrow_pos, own, own_window)
        far_x, far_y = place(wide_pos + move_wide, narrow_pos + move_narrow, far, far_window)
        delta_x = column(own_x) - far_x
        delta_y = column(own_y) - far_y
        square = delta_x * delta_x + delta_y * delta_y
        over = lax.rsqrt(square)
        distance = square * over
        turns = (distance - jnp.round(distance)) * (2.0 * math.pi)
        turns_square = turns * turns
        cosine = horner(taylor(10, 0), turns_square)
        sine = horner(taylor(10, 1), turns_square) * turns
        unit_x = delta_x * over
        unit_y = delta_y * over
        inverse = over * (1.0 / (2.0 * math.pi))
        inverse_square = inverse * inverse
        green = (cosine * inverse, sine * inverse)
        term_a = cmul(green, (1.0 - inverse_square, inverse))
        term_b = cmul(green, (3.0 * inverse_square - 1.0, -3.0 * inverse))
        term_c = (green[0] - green[1] * inverse, green[1] + green[0] * inverse)
        unit_xx = unit_x * unit_x
        unit_xy = unit_x * unit_y
        unit_yy = unit_y * unit_y
        own_mixed = mixed(all_ref[:, own_window])
        far_mixed = mixed(all_ref[:, far_window])
        to_own = jnp.zeros((CHAN, PIL), F32)
        to_far = jnp.zeros((CHAN, PIL), F32)
        for field in range(6):
            for part in range(2):
                value = (
                    term_a[part],
                    term_b[part] * unit_xx,
                    term_b[part] * unit_xy,
                    term_b[part] * unit_yy,
                    term_c[part] * unit_x,
                    term_c[part] * unit_y,
                )[field].astype(BF16)
                rows = slice((field * 2 + part) * CHAN, (field * 2 + part + 1) * CHAN)
                to_own = to_own + dot(far_mixed[rows], value, 1, 1)
                to_far = to_far + dot(own_mixed[rows], value, 1, 0)
        sum_ref[:, own_window] += to_own
        sum_ref[:, far_window] += to_far
        return carry

    lax.fori_loop(0, used, one_slot, 0)
    near_ref[...] = sum_ref[:, 0:WIDTH]
    start = WIDTH
    for back in (back_one, back_two, back_three, back_four):
        width = back.shape[1]
        back[...] = sum_ref[:, start : start + width].astype(BF16)
        start += width


def shape(dims, kind=F32):
    return jax.ShapeDtypeStruct(dims, kind)


def steps(move_wide, move_narrow):
    pairs = []
    for wide in range(N_WIDE):
        for narrow in range(N_NARROW):
            to_wide, to_narrow = wide + move_wide, narrow + move_narrow
            if 0 <= to_wide < N_WIDE and 0 <= to_narrow < N_NARROW:
                pairs.append((wide * N_NARROW + narrow, to_wide * N_NARROW + to_narrow))
    return pairs


MOVES = ((0, 1), (1, 0), (1, -1), (-1, -1))
PARAMS = pltpu.CompilerParams(vmem_limit_bytes=48 * MIB)


def exchange(message):
    code = message * lax.rsqrt(jnp.maximum(jnp.abs(message), 1e-30))
    code = code.reshape(DEVICES, HALF, 128).astype(jnp.float16)
    code = lax.all_to_all(code, AXES, split_axis=0, concat_axis=0, tiled=True)
    code = code.astype(F32)
    return (code * jnp.abs(code)).reshape(DEVICES * HALF, 128)


def local(incident, jitter, weights, cells, pair_list, pair_count, kernel):
    x = incident.reshape(CHAN, WIDTH)
    w = weights.reshape(1, WIDTH)
    cell = cells.reshape(1, WIDTH)

    packed = jnp.concatenate([x, jitter], axis=0)
    pieces = (
        jnp.concatenate([packed[:, c * PIL : (c + 1) * PIL] for c in (0, 4, 8, 12)], axis=1),
        packed[:, 0 : 4 * PIL],
        packed[:, 3 * PIL : 4 * PIL],
        packed[:, 15 * PIL : 16 * PIL],
    )
    halo = [
        lax.ppermute(piece, AXES, steps(-wide, -narrow)) for piece, (wide, narrow) in zip(pieces, MOVES)
    ]

    message = pl.pallas_call(
        rows_kernel,
        out_shape=shape((DEVICES * HALF, 128)),
        scratch_shapes=[
            pltpu.VMEM((1536, WIDTH), BF16),
            pltpu.VMEM((2, 256, WIDTH), BF16),
            pltpu.VMEM((1536, 256), F32),
            pltpu.VMEM((1536, 256), F32),
        ],
        compiler_params=PARAMS,
        cost_estimate=pl.CostEstimate(flops=3_800_000_000, bytes_accessed=4 * MIB, transcendentals=0),
    )(x, w, cell, jnp.asarray(dft_table(-1.0)), jnp.asarray(row_twiddle()))
    columns = exchange(message)

    spots = jnp.concatenate(
        [
            pair_list.reshape(PAIRS * 3),
            lax.axis_index("wide").reshape(1),
            lax.axis_index("narrow").reshape(1),
            pair_count,
        ]
    )
    near, *returns = pl.pallas_call(
        near_kernel,
        in_specs=[pl.BlockSpec(memory_space=pltpu.SMEM)] + [pl.BlockSpec(memory_space=pltpu.VMEM)] * 11,
        out_shape=[
            shape((CHAN, WIDTH)),
            shape((CHAN, 4 * PIL), BF16),
            shape((CHAN, 4 * PIL), BF16),
            shape((CHAN, PIL), BF16),
            shape((CHAN, PIL), BF16),
        ],
        scratch_shapes=[
            pltpu.VMEM((CHAN, WIDTH + HALO * PIL), BF16),
            pltpu.VMEM((8, WIDTH + HALO * PIL), F32),
            pltpu.VMEM((CHAN, WIDTH + HALO * PIL), F32),
        ],
        compiler_params=PARAMS,
        cost_estimate=pl.CostEstimate(flops=8_000_000_000, bytes_accessed=4 * MIB, transcendentals=0),
    )(spots, x, *[h[:CHAN] for h in halo], jitter, *[h[CHAN:] for h in halo], jnp.asarray(mixing_table()))
    back = [
        lax.ppermute(piece, AXES, steps(wide, narrow)) for piece, (wide, narrow) in zip(returns, MOVES)
    ]

    transfer = kernel.reshape(2, 2, 4, 128, 8).transpose(0, 2, 3, 1, 4)
    transfer = jnp.broadcast_to(transfer[..., None], (2, 4, 128, 2, 8, 8)).reshape(2, 512, 128)
    message = pl.pallas_call(
        columns_kernel,
        out_shape=shape((DEVICES * HALF, 128)),
        scratch_shapes=[pltpu.VMEM((256, 1536), F32), pltpu.VMEM((256, 1536), F32)],
        compiler_params=PARAMS,
        cost_estimate=pl.CostEstimate(flops=2_000_000_000, bytes_accessed=6 * MIB, transcendentals=0),
    )(
        columns,
        transfer,
        jnp.asarray(dft_table(-1.0)),
        jnp.asarray(dft_table(1.0, 1.0 / 1048576)),
        jnp.asarray(column_twiddle()),
        jnp.asarray(lane_twiddle()),
    )
    rows = exchange(message)

    coupled = pl.pallas_call(
        sample_kernel,
        out_shape=shape((CHAN, WIDTH)),
        scratch_shapes=[
            pltpu.VMEM((1536, 256), F32),
            pltpu.VMEM((1536, 256), F32),
            pltpu.VMEM((2, 1536, 256), BF16),
        ],
        compiler_params=PARAMS,
        cost_estimate=pl.CostEstimate(flops=3_800_000_000, bytes_accessed=4 * MIB, transcendentals=0),
    )(rows, w, cell, near, *back, jnp.asarray(dft_table(1.0)), jnp.asarray(row_twiddle()))
    return coupled.reshape(2, ANG, 6, WIDTH)


def solution(mesh):
    in_specs = (
        P(None, None, None, AXES),
        P(None, AXES),
        P(AXES),
        P(AXES),
        P(AXES, None, None),
        P(AXES),
        P(None, None, AXES),
    )
    return jax.shard_map(
        local, mesh=mesh, in_specs=in_specs, out_specs=P(None, None, None, AXES), check_vma=False
    )
```

```python
import math

import jax
import jax.numpy as jnp
import numpy as np
from jax import lax
from jax.experimental import pallas as pl
from jax.experimental.pallas import tpu as pltpu
from jax.sharding import PartitionSpec as P

ANG = 4
PCX = 8
PCY = 16
CCX = 4
CCY = 4
PIL = 128
CHAN = 48
HALF = 24
WIDTH = 2048
PAIRS = 8
N_WIDE = 16
N_NARROW = 8
DEVICES = 128
AXES = ("wide", "narrow")
PITCH = 0.4
BF16 = jnp.bfloat16
F32 = jnp.float32
HALO = 10
MIB = 1 << 20


def split_table(table):
    high = table.astype(BF16)
    low = (table - high.astype(np.float64)).astype(BF16)
    return np.stack([high, low])


def dft_table(sign, scale=1.0):
    ids = np.arange(128)
    angles = (ids[:, None] * ids[None, :] % 128) * (2.0 * math.pi / 128)
    cosine = np.cos(angles) * scale
    sine = np.sin(angles) * scale * sign
    return split_table(np.block([[cosine, -sine], [sine, cosine]]))


def row_twiddle():
    k1 = np.repeat(np.arange(8), 8)
    angles = (k1[:, None] * np.arange(128)[None, :]) * (2.0 * math.pi / 1024)
    return np.stack([np.cos(angles), -np.sin(angles)]).astype(np.float32)


def column_twiddle():
    row = (np.arange(128) // 64)[None, None, :] + 2 * np.arange(4)[:, None, None]
    angles = (row * np.arange(128)[None, :, None]) * (2.0 * math.pi / 1024)
    return np.stack([np.cos(angles), -np.sin(angles)]).reshape(2, 512, 128).astype(np.float32)


def lane_twiddle():
    side = (np.arange(128) // 64)[None, :]
    angles = np.arange(4)[:, None] * side * (2.0 * math.pi / 8)
    table = np.concatenate([np.cos(angles), -np.sin(angles), np.where(side == 0, 1.0, -1.0)])
    return np.concatenate([table, np.zeros((7, 128))]).astype(np.float32)


def mixing_table():
    table = np.zeros((6, 6, 6), np.float32)
    for member in range(6):
        table[0, member, member] = 1.0
    for offset in (0, 3):
        table[1, offset, offset] = 1.0
        table[2, offset, offset + 1] = 1.0
        table[2, offset + 1, offset] = 1.0
        table[3, offset + 1, offset + 1] = 1.0
    table[4, 2, 4] = 1.0
    table[4, 4, 2] = 1.0
    table[4, 1, 5] = -1.0
    table[4, 5, 1] = -1.0
    table[5, 0, 5] = 1.0
    table[5, 5, 0] = 1.0
    table[5, 2, 3] = -1.0
    table[5, 3, 2] = -1.0
    parts = np.zeros((2, 2, 2), np.float32)
    parts[0] = np.eye(2)
    parts[1] = np.array([[0.0, -1.0], [1.0, 0.0]])
    full = np.einsum("fab,rop,gh->froagpbh", table, parts, np.eye(ANG))
    return full.reshape(12 * CHAN, CHAN).astype(BF16)


def dot(left, right, left_dim=1, right_dim=0):
    return lax.dot_general(
        left, right, (((left_dim,), (right_dim,)), ((), ())), preferred_element_type=F32
    )


def halves(value):
    high = value.astype(BF16)
    return high, (value - high.astype(F32)).astype(BF16)


def cadd(left, right):
    return (left[0] + right[0], left[1] + right[1])


def csub(left, right):
    return (left[0] - right[0], left[1] - right[1])


def cmul(left, right):
    return (left[0] * right[0] - left[1] * right[1], left[0] * right[1] + left[1] * right[0])


def cmul_conj(left, right):
    return (left[0] * right[0] + left[1] * right[1], left[1] * right[0] - left[0] * right[1])


def turn(value, sign):
    if sign < 0:
        return (value[1], -value[0])
    return (-value[1], value[0])


def dft4(values, sign):
    even, odd = cadd(values[0], values[2]), csub(values[0], values[2])
    left, right = cadd(values[1], values[3]), turn(csub(values[1], values[3]), sign)
    return [cadd(even, left), cadd(odd, right), csub(even, left), csub(odd, right)]


def dft8(values, sign):
    even = dft4(values[0::2], sign)
    odd = dft4(values[1::2], sign)
    root = math.sqrt(0.5)
    first, third = odd[1], odd[3]
    odd[1] = ((first[0] - sign * first[1]) * root, (first[1] + sign * first[0]) * root)
    odd[2] = turn(odd[2], sign)
    odd[3] = ((-third[0] - sign * third[1]) * root, (-third[1] + sign * third[0]) * root)
    return [cadd(e, o) for e, o in zip(even, odd)] + [csub(e, o) for e, o in zip(even, odd)]


def pack_kernel(x_ref, jitter_ref, own_ref, one_ref, two_ref, four_ref, pack_ref):
    for slab in range(12):
        pack_ref[slab * 4 : slab * 4 + 4, :] = x_ref[slab].astype(F32)
    pack_ref[CHAN : CHAN + 16, :] = jnp.zeros((16, WIDTH), F32)
    pack_ref[CHAN : CHAN + 2, :] = jitter_ref[...].astype(F32)
    own_ref[...] = pack_ref[...].astype(BF16)
    for cluster in range(4):
        one_ref[:, cluster * PIL : (cluster + 1) * PIL] = own_ref[:, cluster * 4 * PIL : (cluster * 4 + 1) * PIL]
    two_ref[...] = own_ref[:, 0 : 4 * PIL]
    four_ref[...] = own_ref[:, 15 * PIL : 16 * PIL]


def rows_kernel(
    x_ref, w_ref, cell_ref, dft_ref, tw_ref, out_ref, pack_ref, xb_ref, xt_ref, hot_ref, g_ref, b_ref
):
    for slab in range(12):
        pack_ref[slab * 4 : slab * 4 + 4, :] = x_ref[slab].astype(F32)
    xb_ref[...] = pack_ref[...].astype(BF16)
    cells = cell_ref[...]
    upper = cells >> 8
    weight = w_ref[...]
    high = weight.astype(BF16).astype(F32)
    low = weight - high
    for block in range(16):
        place = lax.broadcasted_iota(jnp.int32, (16, WIDTH), 0) + block * 16
        hit = place == (cells & 255)
        hot_ref[0, block * 16 : block * 16 + 16, :] = jnp.where(hit, high, 0.0).astype(BF16)
        hot_ref[1, block * 16 : block * 16 + 16, :] = jnp.where(hit, low, 0.0).astype(BF16)
    for part in range(32):
        mask = jnp.where(upper == part, 1.0, 0.0).astype(BF16)
        xt_ref[part * CHAN : (part + 1) * CHAN, :] = xb_ref[...] * mask
    for chunk in range(2):
        rows = slice(chunk * 768, (chunk + 1) * 768)
        piece = xt_ref[rows, :]
        g_ref[rows, :] = dot(piece, hot_ref[0], 1, 1) + dot(piece, hot_ref[1], 1, 1)

    def one_row(row, carry):
        for t in range(3):
            values = []
            for n1 in range(8):
                start = (row * 4 + n1 // 2) * CHAN + t * 8
                lanes = slice((n1 % 2) * 128, (n1 % 2) * 128 + 128)
                values.append(
                    (
                        g_ref[pl.ds(pl.multiple_of(start, 8), 8), lanes],
                        g_ref[pl.ds(pl.multiple_of(start + HALF, 8), 8), lanes],
                    )
                )
            values = dft8(values, -1.0)
            base = (((row // 2) * 3 + t) * 2 + row % 2) * 64
            for k1 in range(8):
                value = values[k1]
                if k1 > 0:
                    twiddle = (
                        tw_ref[0, k1 * 8 : k1 * 8 + 8, :],
                        tw_ref[1, k1 * 8 : k1 * 8 + 8, :],
                    )
                    value = cmul(value, twiddle)
                rows = pl.ds(pl.multiple_of(base + k1 * 8, 8), 8)
                b_ref[rows, 0:128] = value[0]
                b_ref[rows, 128:256] = value[1]
        return carry

    lax.fori_loop(0, 8, one_row, 0)
    for pair in range(6):
        b_high, b_low = halves(b_ref[pair * 256 : (pair + 1) * 256, :])
        result = (
            dot(dft_ref[0], b_high, 1, 1) + dot(dft_ref[0], b_low, 1, 1) + dot(dft_ref[1], b_high, 1, 1)
        )
        for part in range(2):
            for side in range(2):
                out_ref[pl.ds(part * 12 + pair * 2 + side, 128, 24), :] = result[
                    part * 128 : (part + 1) * 128, side * 128 : (side + 1) * 128
                ]


def columns_kernel(r_ref, kern_ref, fwd_ref, inv_ref, tw_ref, lane_ref, out_ref, v_ref, u_ref):
    for part in range(2):
        for group in range(12):
            v_ref[part * 128 : (part + 1) * 128, group * 128 : (group + 1) * 128] = r_ref[
                pl.ds(part * 12 + group, 128, 24), :
            ]
    for chunk in range(6):
        lanes = slice(chunk * 256, (chunk + 1) * 256)
        v_high, v_low = halves(v_ref[:, lanes])
        u_ref[:, lanes] = dot(fwd_ref[0], v_high) + dot(fwd_ref[0], v_low) + dot(fwd_ref[1], v_high)
    sign = lane_ref[8:9, :]

    def swap(value):
        return tuple(part * sign + pltpu.roll(part, 64, 1) for part in value)

    def one_block(block, carry):
        start = pl.multiple_of(block * 8, 8)
        re_rows = pl.ds(start, 8)
        im_rows = pl.ds(pl.multiple_of(start + 128, 8), 8)
        twiddles, kernels = [], []
        for m in range(4):
            rows = pl.ds(pl.multiple_of(start + m * 128, 8), 8)
            twiddles.append((tw_ref[0, rows, :], tw_ref[1, rows, :]))
            kernels.append((kern_ref[0, rows, :], kern_ref[1, rows, :]))
        for t in range(3):
            values = []
            for m in range(4):
                lanes = slice((m * 3 + t) * 128, (m * 3 + t + 1) * 128)
                values.append(cmul((u_ref[re_rows, lanes], u_ref[im_rows, lanes]), twiddles[m]))
            values = dft4(values, -1.0)
            for a in range(4):
                side = (lane_ref[a : a + 1, :], lane_ref[4 + a : 5 + a, :])
                value = values[a] if a == 0 else cmul(values[a], side)
                value = swap(cmul(swap(value), kernels[a]))
                values[a] = value if a == 0 else cmul_conj(value, side)
            values = dft4(values, 1.0)
            for m in range(4):
                lanes = slice((m * 3 + t) * 128, (m * 3 + t + 1) * 128)
                value = cmul_conj(values[m], twiddles[m])
                v_ref[re_rows, lanes] = value[0]
                v_ref[im_rows, lanes] = value[1]
        return carry

    lax.fori_loop(0, 16, one_block, 0)
    for chunk in range(6):
        lanes = slice(chunk * 256, (chunk + 1) * 256)
        v_high, v_low = halves(v_ref[:, lanes])
        result = dot(inv_ref[0], v_high) + dot(inv_ref[0], v_low) + dot(inv_ref[1], v_high)
        for part in range(2):
            for side in range(2):
                out_ref[pl.ds(part * 12 + chunk * 2 + side, 128, 24), :] = result[
                    part * 128 : (part + 1) * 128, side * 128 : (side + 1) * 128
                ]


def sample_kernel(
    r_ref, w_ref, cell_ref, near_ref, both_ref, side_ref, four_ref, dft_ref, tw_ref,
    out_ref, v_ref, g_ref, f_ref, sum_ref,
):
    for part in range(2):
        for group in range(12):
            piece = r_ref[pl.ds(part * 12 + group, 128, 24), :]
            v_ref[group * 128 : (group + 1) * 128, part * 128 : (part + 1) * 128] = piece.T
    for chunk in range(2):
        rows = slice(chunk * 768, (chunk + 1) * 768)
        v_high, v_low = halves(v_ref[rows, :])
        g_ref[rows, :] = (
            dot(v_high, dft_ref[0], 1, 1) + dot(v_low, dft_ref[0], 1, 1) + dot(v_high, dft_ref[1], 1, 1)
        )

    def one_row(row, carry):
        for t in range(3):
            base = (((row // 2) * 3 + t) * 2 + row % 2) * 64
            values = []
            for k1 in range(8):
                rows = pl.ds(pl.multiple_of(base + k1 * 8, 8), 8)
                value = (g_ref[rows, 0:128], g_ref[rows, 128:256])
                if k1 > 0:
                    twiddle = (
                        tw_ref[0, k1 * 8 : k1 * 8 + 8, :],
                        tw_ref[1, k1 * 8 : k1 * 8 + 8, :],
                    )
                    value = cmul_conj(value, twiddle)
                values.append(value)
            values = dft8(values, 1.0)
            for n1 in range(8):
                start = (row * 4 + n1 // 2) * CHAN + t * 8
                lanes = slice((n1 % 2) * 128, (n1 % 2) * 128 + 128)
                v_ref[pl.ds(pl.multiple_of(start, 8), 8), lanes] = values[n1][0]
                v_ref[pl.ds(pl.multiple_of(start + HALF, 8), 8), lanes] = values[n1][1]
        return carry

    lax.fori_loop(0, 8, one_row, 0)
    f_high, f_low = halves(v_ref[...])
    f_ref[0] = f_high
    f_ref[1] = f_low
    place = lax.broadcasted_iota(jnp.int32, (256, 256), 0)
    for chunk in range(8):
        lanes = slice(chunk * 256, (chunk + 1) * 256)
        cells = cell_ref[:, lanes]
        hot = jnp.where(place == (cells & 255), 1.0, 0.0).astype(BF16)
        upper = cells >> 8
        total = jnp.zeros((CHAN, 256), F32)
        for quarter in range(4):
            rows = slice(quarter * 384, (quarter + 1) * 384)
            picked = dot(f_ref[0, rows, :], hot) + dot(f_ref[1, rows, :], hot)
            for part in range(8):
                hit = jnp.broadcast_to(upper == quarter * 8 + part, (CHAN, 256))
                total = total + jnp.where(hit, picked[part * CHAN : (part + 1) * CHAN, :], 0.0)
        sum_ref[:, lanes] = total * w_ref[:, lanes] + near_ref[:, lanes]
    for cluster in range(4):
        lanes = slice(cluster * 4 * PIL, (cluster * 4 + 1) * PIL)
        sum_ref[:, lanes] += both_ref[:, cluster * PIL : (cluster + 1) * PIL].astype(F32)
        lanes = slice(cluster * PIL, (cluster + 1) * PIL)
        sum_ref[:, lanes] += both_ref[:, (cluster + 4) * PIL : (cluster + 5) * PIL].astype(F32)
    sum_ref[:, 3 * PIL : 4 * PIL] += side_ref[:, 4 * PIL : 5 * PIL].astype(F32)
    sum_ref[:, 15 * PIL : 16 * PIL] += four_ref[...].astype(F32)
    for slab in range(12):
        out_ref[slab] = sum_ref[slab * 4 : slab * 4 + 4, :]


def taylor(count, first):
    return [(-1.0) ** n / math.factorial(2 * n + first) for n in range(count)]


def horner(coefficients, square):
    total = jnp.full_like(square, coefficients[-1])
    for coefficient in coefficients[-2::-1]:
        total = total * square + coefficient
    return total


def near_kernel(
    list_ref, own_ref, both_ref, side_ref, four_ref, mix_ref,
    near_ref, back_one, back_side, back_four, all_ref, pos_ref, sum_ref,
):
    start = 0
    for data in (own_ref[...], both_ref[...], side_ref[:, 3 * PIL : 4 * PIL], four_ref[...]):
        width = data.shape[1]
        all_ref[:, start : start + width] = data[0:CHAN, :]
        pos_ref[:, start : start + width] = data[CHAN : CHAN + 16, :].astype(F32)
        start += width
    sum_ref[...] = jnp.zeros_like(sum_ref)
    wide_pos = list_ref[24]
    narrow_pos = list_ref[25]
    used = list_ref[26]
    local = lax.broadcasted_iota(jnp.int32, (1, PIL), 1)

    def place(wide, narrow, cluster, window):
        across = ((wide * CCX + cluster // CCY) * PCX + local // PCY).astype(F32)
        along = ((narrow * CCY + cluster % CCY) * PCY + local % PCY).astype(F32)
        return across * PITCH + pos_ref[0:1, window], along * PITCH + pos_ref[1:2, window]

    def column(vector):
        return jnp.broadcast_to(vector, (PIL, PIL)).T

    def mixed(values):
        return dot(mix_ref[...], values).astype(BF16)

    def one_slot(slot):
        direction = list_ref[slot * 3]
        own = list_ref[slot * 3 + 1]
        far = list_ref[slot * 3 + 2]
        move_wide = jnp.where(direction == 4, -1, jnp.where(direction >= 2, 1, 0))
        move_narrow = jnp.where(direction == 1, 1, jnp.where(direction >= 3, -1, 0))
        index = jnp.where(direction == 1, 16 + far // 4, far)
        index = jnp.where(direction == 2, 20 + far, index)
        index = jnp.where(direction == 3, 24, index)
        index = jnp.where(direction == 4, 25, index)
        own_window = pl.ds(pl.multiple_of(own * PIL, PIL), PIL)
        far_window = pl.ds(pl.multiple_of(index * PIL, PIL), PIL)
        own_x, own_y = place(wide_pos, narrow_pos, own, own_window)
        far_x, far_y = place(wide_pos + move_wide, narrow_pos + move_narrow, far, far_window)
        delta_x = column(own_x) - far_x
        delta_y = column(own_y) - far_y
        square = delta_x * delta_x + delta_y * delta_y
        over = lax.rsqrt(square)
        distance = square * over
        half_turns = (distance - jnp.round(distance)) * math.pi
        half_square = half_turns * half_turns
        half_sine = horner(taylor(7, 1), half_square) * half_turns
        half_cosine = horner(taylor(8, 0), half_square)
        cosine = 1.0 - 2.0 * half_sine * half_sine
        sine = 2.0 * half_sine * half_cosine
        unit_x = delta_x * over
        unit_y = delta_y * over
        inverse = over * (1.0 / (2.0 * math.pi))
        inverse_square = inverse * inverse
        green = (cosine * inverse, sine * inverse)
        term_a = cmul(green, (1.0 - inverse_square, inverse))
        term_b = cmul(green, (3.0 * inverse_square - 1.0, -3.0 * inverse))
        term_c = (green[0] - green[1] * inverse, green[1] + green[0] * inverse)
        unit_xx = unit_x * unit_x
        unit_xy = unit_x * unit_y
        unit_yy = unit_y * unit_y
        own_mixed = mixed(all_ref[:, own_window])
        far_mixed = mixed(all_ref[:, far_window])
        fields = []
        for field in range(6):
            for part in range(2):
                value = (
                    term_a[part],
                    term_b[part] * unit_xx,
                    term_b[part] * unit_xy,
                    term_b[part] * unit_yy,
                    term_c[part] * unit_x,
                    term_c[part] * unit_y,
                )[field].astype(BF16)
                fields.append(value)
        far_wide = jnp.concatenate([far_mixed[k * CHAN : (k + 1) * CHAN] for k in range(12)], axis=1)
        own_wide = jnp.concatenate([own_mixed[k * CHAN : (k + 1) * CHAN] for k in range(12)], axis=1)
        to_own = dot(far_wide, jnp.concatenate(fields, axis=1), 1, 1)
        to_far = dot(own_wide, jnp.concatenate(fields, axis=0), 1, 0)
        active = jnp.where(slot < used, 1.0, 0.0)
        return own_window, far_window, to_own * active, to_far * active

    def some_slots(step, carry):
        results = [one_slot(step * 4 + place) for place in range(4)]
        for own_window, far_window, to_own, to_far in results:
            sum_ref[:, own_window] += to_own
            sum_ref[:, far_window] += to_far
        return carry

    lax.fori_loop(0, (used + 3) // 4, some_slots, 0)
    near_ref[...] = sum_ref[:, 0:WIDTH]
    start = WIDTH
    for back in (back_one, back_side, back_four):
        width = back.shape[1]
        back[...] = sum_ref[:, start : start + width].astype(BF16)
        start += width


def shape(dims, kind=F32):
    return jax.ShapeDtypeStruct(dims, kind)


def shift(value, move_wide, move_narrow):
    pairs = []
    for wide in range(N_WIDE):
        for narrow in range(N_NARROW):
            to_wide, to_narrow = wide + move_wide, (narrow + move_narrow) % N_NARROW
            if 0 <= to_wide < N_WIDE:
                pairs.append((wide * N_NARROW + narrow, to_wide * N_NARROW + to_narrow))
    return lax.ppermute(value, AXES, pairs)


PARAMS = pltpu.CompilerParams(vmem_limit_bytes=48 * MIB)


def cost(flops, size):
    return pl.CostEstimate(flops=flops, bytes_accessed=size, transcendentals=0)


def pack_call(x, jitter):
    return pl.pallas_call(
        pack_kernel,
        out_shape=[
            shape((64, WIDTH), BF16),
            shape((64, 4 * PIL), BF16),
            shape((64, 4 * PIL), BF16),
            shape((64, PIL), BF16),
        ],
        scratch_shapes=[pltpu.VMEM((64, WIDTH), F32)],
        compiler_params=PARAMS,
        cost_estimate=cost(1_000_000, MIB // 2),
    )(x, jitter)


def rows_call(x, w, cell, forward, row_table):
    return pl.pallas_call(
        rows_kernel,
        out_shape=shape((DEVICES * HALF, 128)),
        scratch_shapes=[
            pltpu.VMEM((CHAN, WIDTH), F32),
            pltpu.VMEM((CHAN, WIDTH), BF16),
            pltpu.VMEM((1536, WIDTH), BF16),
            pltpu.VMEM((2, 256, WIDTH), BF16),
            pltpu.VMEM((1536, 256), F32),
            pltpu.VMEM((1536, 256), F32),
        ],
        compiler_params=PARAMS,
        cost_estimate=cost(3_800_000_000, 4 * MIB),
    )(x, w, cell, forward, row_table)


def near_call(spots, own, both, side, four, mixing):
    return pl.pallas_call(
        near_kernel,
        in_specs=[pl.BlockSpec(memory_space=pltpu.SMEM)] + [pl.BlockSpec(memory_space=pltpu.VMEM)] * 5,
        out_shape=[
            shape((CHAN, WIDTH)),
            shape((CHAN, 4 * PIL), BF16),
            shape((CHAN, 5 * PIL), BF16),
            shape((CHAN, PIL), BF16),
        ],
        scratch_shapes=[
            pltpu.VMEM((CHAN, WIDTH + HALO * PIL), BF16),
            pltpu.VMEM((16, WIDTH + HALO * PIL), F32),
            pltpu.VMEM((CHAN, WIDTH + HALO * PIL), F32),
        ],
        compiler_params=PARAMS,
        cost_estimate=cost(8_000_000_000, 4 * MIB),
    )(spots, own, both, side, four, mixing)


def columns_call(columns, transfer, forward, backward, column_table, lane_table):
    return pl.pallas_call(
        columns_kernel,
        out_shape=shape((DEVICES * HALF, 128)),
        scratch_shapes=[pltpu.VMEM((256, 1536), F32), pltpu.VMEM((256, 1536), F32)],
        compiler_params=PARAMS,
        cost_estimate=cost(2_000_000_000, 6 * MIB),
    )(columns, transfer, forward, backward, column_table, lane_table)


def sample_call(rows, w, cell, near, both, side, four, backward, row_table):
    return pl.pallas_call(
        sample_kernel,
        out_shape=shape((12, 4, WIDTH)),
        scratch_shapes=[
            pltpu.VMEM((1536, 256), F32),
            pltpu.VMEM((1536, 256), F32),
            pltpu.VMEM((2, 1536, 256), BF16),
            pltpu.VMEM((CHAN, WIDTH), F32),
        ],
        compiler_params=PARAMS,
        cost_estimate=cost(3_800_000_000, 4 * MIB),
    )(rows, w, cell, near, both, side, four, backward, row_table)


def exchange(message):
    code = message * lax.rsqrt(jnp.maximum(jnp.abs(message), 1e-30))
    code = code.reshape(DEVICES, HALF, 128).astype(jnp.float16)
    code = lax.all_to_all(code, AXES, split_axis=0, concat_axis=0, tiled=True)
    code = code.astype(F32)
    return (code * jnp.abs(code)).reshape(DEVICES * HALF, 128)


def local(incident, jitter, weights, cells, pair_list, pair_count, kernel):
    x = incident.transpose(0, 2, 1, 3).reshape(12, ANG, WIDTH)
    w = weights.reshape(1, WIDTH)
    cell = cells.reshape(1, WIDTH)
    forward = jnp.asarray(dft_table(-1.0))
    row_table = jnp.asarray(row_twiddle())

    message = rows_call(x, w, cell, forward, row_table)
    columns = exchange(message)
    own, one, two, four = pack_call(x, jitter)
    side = shift(two, -1, 1)
    four = shift(four, 1, 1)
    both = shift(jnp.concatenate([one, side], axis=1), 0, -1)

    transfer = kernel.reshape(2, 2, 4, 128, 8).transpose(0, 2, 3, 1, 4)
    transfer = jnp.broadcast_to(transfer[..., None], (2, 4, 128, 2, 8, 8)).reshape(2, 512, 128)
    message = columns_call(
        columns,
        transfer,
        forward,
        jnp.asarray(dft_table(1.0, 1.0 / 1048576)),
        jnp.asarray(column_twiddle()),
        jnp.asarray(lane_twiddle()),
    )
    rows = exchange(message)

    spots = jnp.concatenate(
        [
            pair_list.reshape(PAIRS * 3),
            lax.axis_index("wide").reshape(1),
            lax.axis_index("narrow").reshape(1),
            pair_count,
        ]
    )
    near, one, side, four = near_call(spots, own, both, side, four, jnp.asarray(mixing_table()))
    side = shift(side, 1, -1)
    four = shift(four, -1, -1)
    both = shift(jnp.concatenate([one, side[:, 0 : 4 * PIL]], axis=1), 0, 1)
    coupled = sample_call(rows, w, cell, near, both, side, four, jnp.asarray(dft_table(1.0)), row_table)
    return coupled.reshape(2, 6, ANG, WIDTH).transpose(0, 2, 1, 3)


def solution(mesh):
    in_specs = (
        P(None, None, None, AXES),
        P(None, AXES),
        P(AXES),
        P(AXES),
        P(AXES, None, None),
        P(AXES),
        P(None, None, AXES),
    )
    return jax.shard_map(
        local, mesh=mesh, in_specs=in_specs, out_specs=P(None, None, None, AXES), check_vma=False
    )
```

```python
import math

import jax
import jax.numpy as jnp
import numpy as np
from jax import lax
from jax.experimental import pallas as pl
from jax.experimental.pallas import tpu as pltpu
from jax.sharding import PartitionSpec as P

ANG = 4
PCX = 8
PCY = 16
CCX = 4
CCY = 4
PIL = 128
CHAN = 48
HALF = 24
WIDTH = 2048
PAIRS = 8
N_WIDE = 16
N_NARROW = 8
DEVICES = 128
AXES = ("wide", "narrow")
PITCH = 0.4
BF16 = jnp.bfloat16
F32 = jnp.float32
HALO = 10
MIB = 1 << 20


def split_table(table):
    high = table.astype(BF16)
    low = (table - high.astype(np.float64)).astype(BF16)
    return np.stack([high, low])


def dft_table(sign, scale=1.0):
    ids = np.arange(128)
    angles = (ids[:, None] * ids[None, :] % 128) * (2.0 * math.pi / 128)
    cosine = np.cos(angles) * scale
    sine = np.sin(angles) * scale * sign
    return split_table(np.block([[cosine, -sine], [sine, cosine]]))


def row_table():
    k1 = np.repeat(np.arange(8), 8)
    angles = (k1[:, None] * np.arange(128)[None, :]) * (2.0 * math.pi / 1024)
    twiddle = split_table(np.concatenate([np.cos(angles), -np.sin(angles)]))
    return np.concatenate([*dft_table(-1.0), np.concatenate([*twiddle], axis=1)])


def column_twiddle():
    row = (np.arange(128) // 64)[None, None, :] + 2 * np.arange(4)[:, None, None]
    angles = (row * np.arange(128)[None, :, None]) * (2.0 * math.pi / 1024)
    return np.stack([np.cos(angles), -np.sin(angles)]).reshape(2, 512, 128).astype(np.float32)


def lane_twiddle():
    side = (np.arange(128) // 64)[None, :]
    angles = np.arange(4)[:, None] * side * (2.0 * math.pi / 8)
    table = np.concatenate([np.cos(angles), -np.sin(angles), np.where(side == 0, 1.0, -1.0)])
    return np.concatenate([table, np.zeros((7, 128))]).astype(np.float32)


def mixing_table():
    table = np.zeros((6, 6, 6), np.float32)
    for member in range(6):
        table[0, member, member] = 1.0
    for offset in (0, 3):
        table[1, offset, offset] = 1.0
        table[2, offset, offset + 1] = 1.0
        table[2, offset + 1, offset] = 1.0
        table[3, offset + 1, offset + 1] = 1.0
    table[4, 2, 4] = 1.0
    table[4, 4, 2] = 1.0
    table[4, 1, 5] = -1.0
    table[4, 5, 1] = -1.0
    table[5, 0, 5] = 1.0
    table[5, 5, 0] = 1.0
    table[5, 2, 3] = -1.0
    table[5, 3, 2] = -1.0
    parts = np.zeros((2, 2, 2), np.float32)
    parts[0] = np.eye(2)
    parts[1] = np.array([[0.0, -1.0], [1.0, 0.0]])
    full = np.einsum("fab,rop,gh->froagpbh", table, parts, np.eye(ANG))
    return full.reshape(12 * CHAN, CHAN).astype(BF16)


def dot(left, right, left_dim=1, right_dim=0):
    return lax.dot_general(
        left, right, (((left_dim,), (right_dim,)), ((), ())), preferred_element_type=F32
    )


def halves(value):
    high = value.astype(BF16)
    return high, (value - high.astype(F32)).astype(BF16)


def coded(value):
    return value * lax.rsqrt(jnp.maximum(jnp.abs(value), 1e-30))


def cadd(left, right):
    return (left[0] + right[0], left[1] + right[1])


def csub(left, right):
    return (left[0] - right[0], left[1] - right[1])


def cmul(left, right):
    return (left[0] * right[0] - left[1] * right[1], left[0] * right[1] + left[1] * right[0])


def cmul_conj(left, right):
    return (left[0] * right[0] + left[1] * right[1], left[1] * right[0] - left[0] * right[1])


def turn(value, sign):
    if sign < 0:
        return (value[1], -value[0])
    return (-value[1], value[0])


def dft4(values, sign):
    even, odd = cadd(values[0], values[2]), csub(values[0], values[2])
    left, right = cadd(values[1], values[3]), turn(csub(values[1], values[3]), sign)
    return [cadd(even, left), cadd(odd, right), csub(even, left), csub(odd, right)]


def dft8(values, sign):
    even = dft4(values[0::2], sign)
    odd = dft4(values[1::2], sign)
    root = math.sqrt(0.5)
    first, third = odd[1], odd[3]
    odd[1] = ((first[0] - sign * first[1]) * root, (first[1] + sign * first[0]) * root)
    odd[2] = turn(odd[2], sign)
    odd[3] = ((-third[0] - sign * third[1]) * root, (-third[1] + sign * third[0]) * root)
    return [cadd(e, o) for e, o in zip(even, odd)] + [csub(e, o) for e, o in zip(even, odd)]


def pack_kernel(x_ref, jitter_ref, own_ref, one_ref, two_ref, four_ref, pack_ref):
    for slab in range(12):
        pack_ref[slab * 4 : slab * 4 + 4, :] = x_ref[slab].astype(F32)
    pack_ref[CHAN : CHAN + 16, :] = jnp.zeros((16, WIDTH), F32)
    pack_ref[CHAN : CHAN + 2, :] = jitter_ref[...].astype(F32)
    own_ref[...] = pack_ref[...].astype(BF16)
    for cluster in range(4):
        one_ref[:, cluster * PIL : (cluster + 1) * PIL] = own_ref[:, cluster * 4 * PIL : (cluster * 4 + 1) * PIL]
    two_ref[...] = own_ref[:, 0 : 4 * PIL]
    four_ref[...] = own_ref[:, 15 * PIL : 16 * PIL]


def twiddles(table_ref):
    return table_ref[512:640, 0:128].astype(F32) + table_ref[512:640, 128:256].astype(F32)


def rows_kernel(
    x_ref, w_ref, cell_ref, table_ref, out_ref, pack_ref, xb_ref, xt_ref, hot_ref, g_ref, b_ref, tw_ref
):
    for slab in range(12):
        pack_ref[slab * 4 : slab * 4 + 4, :] = x_ref[slab].astype(F32)
    xb_ref[...] = pack_ref[...].astype(BF16)
    tw_ref[...] = twiddles(table_ref)
    cells = cell_ref[...]
    upper = cells >> 8
    weight = w_ref[...]
    high = weight.astype(BF16).astype(F32)
    low = weight - high
    for block in range(16):
        place = lax.broadcasted_iota(jnp.int32, (16, WIDTH), 0) + block * 16
        hit = place == (cells & 255)
        hot_ref[0, block * 16 : block * 16 + 16, :] = jnp.where(hit, high, 0.0).astype(BF16)
        hot_ref[1, block * 16 : block * 16 + 16, :] = jnp.where(hit, low, 0.0).astype(BF16)
    for part in range(32):
        mask = jnp.where(upper == part, 1.0, 0.0).astype(BF16)
        xt_ref[part * CHAN : (part + 1) * CHAN, :] = xb_ref[...] * mask
    for chunk in range(2):
        rows = slice(chunk * 768, (chunk + 1) * 768)
        piece = xt_ref[rows, :]
        g_ref[rows, :] = dot(piece, hot_ref[0], 1, 1) + dot(piece, hot_ref[1], 1, 1)

    def one_row(row):
        for t in range(3):
            values = []
            for n1 in range(8):
                start = (row * 4 + n1 // 2) * CHAN + t * 8
                lanes = slice((n1 % 2) * 128, (n1 % 2) * 128 + 128)
                values.append(
                    (
                        g_ref[pl.ds(pl.multiple_of(start, 8), 8), lanes],
                        g_ref[pl.ds(pl.multiple_of(start + HALF, 8), 8), lanes],
                    )
                )
            values = dft8(values, -1.0)
            base = (((row // 2) * 3 + t) * 2 + row % 2) * 64
            for k1 in range(8):
                value = values[k1]
                if k1 > 0:
                    twiddle = (
                        tw_ref[0 + k1 * 8 : 8 + k1 * 8, :],
                        tw_ref[64 + k1 * 8 : 72 + k1 * 8, :],
                    )
                    value = cmul(value, twiddle)
                rows = pl.ds(pl.multiple_of(base + k1 * 8, 8), 8)
                b_ref[rows, 0:128] = value[0]
                b_ref[rows, 128:256] = value[1]

    for row in range(8):
        one_row(row)
    for pair in range(6):
        b_high, b_low = halves(b_ref[pair * 256 : (pair + 1) * 256, :])
        result = (
            dot(table_ref[0:256, :], b_high, 1, 1)
            + dot(table_ref[0:256, :], b_low, 1, 1)
            + dot(table_ref[256:512, :], b_high, 1, 1)
        )
        result = coded(result)
        for part in range(2):
            for side in range(2):
                out_ref[pl.ds(part * 12 + pair * 2 + side, 128, 24), :] = result[
                    part * 128 : (part + 1) * 128, side * 128 : (side + 1) * 128
                ]


def columns_kernel(r_ref, kern_ref, fwd_ref, inv_ref, tw_ref, lane_ref, out_ref, v_ref, u_ref, y_ref):
    sign = lane_ref[8:9, :]

    def swap(value):
        return tuple(part * sign + pltpu.roll(part, 64, 1) for part in value)

    def lanes_of(t, m):
        return slice((t * 4 + m) * 128, (t * 4 + m + 1) * 128)

    def spread(t):
        for part in range(2):
            for m in range(4):
                v_ref[part * 128 : (part + 1) * 128, lanes_of(t, m)] = r_ref[
                    pl.ds(part * 12 + m * 3 + t, 128, 24), :
                ]
        for chunk in range(2):
            lanes = slice((t * 2 + chunk) * 256, (t * 2 + chunk + 1) * 256)
            v_high, v_low = halves(v_ref[:, lanes])
            u_ref[:, lanes] = dot(fwd_ref[0], v_high) + dot(fwd_ref[0], v_low) + dot(fwd_ref[1], v_high)

    def multiply(t):
        for block in range(16):
            re_rows = slice(block * 8, block * 8 + 8)
            im_rows = slice(block * 8 + 128, block * 8 + 136)
            values, twiddles = [], []
            for m in range(4):
                rows = slice(m * 128 + block * 8, m * 128 + block * 8 + 8)
                twiddles.append((tw_ref[0, rows, :], tw_ref[1, rows, :]))
                lanes = lanes_of(t, m)
                values.append(cmul((u_ref[re_rows, lanes], u_ref[im_rows, lanes]), twiddles[m]))
            values = dft4(values, -1.0)
            for a in range(4):
                rows = slice(a * 128 + block * 8, a * 128 + block * 8 + 8)
                side = (lane_ref[a : a + 1, :], lane_ref[4 + a : 5 + a, :])
                value = values[a] if a == 0 else cmul(values[a], side)
                value = swap(cmul(swap(value), (kern_ref[0, rows, :], kern_ref[1, rows, :])))
                values[a] = value if a == 0 else cmul_conj(value, side)
            values = dft4(values, 1.0)
            for m in range(4):
                value = cmul_conj(values[m], twiddles[m])
                y_ref[re_rows, lanes_of(t, m)] = value[0]
                y_ref[im_rows, lanes_of(t, m)] = value[1]

    def gather(t):
        for chunk in range(2):
            lanes = slice((t * 2 + chunk) * 256, (t * 2 + chunk + 1) * 256)
            y_high, y_low = halves(y_ref[:, lanes])
            result = coded(dot(inv_ref[0], y_high) + dot(inv_ref[0], y_low) + dot(inv_ref[1], y_high))
            for part in range(2):
                for side in range(2):
                    out_ref[pl.ds(part * 12 + (chunk * 2 + side) * 3 + t, 128, 24), :] = result[
                        part * 128 : (part + 1) * 128, side * 128 : (side + 1) * 128
                    ]

    spread(0)
    spread(1)
    multiply(0)
    spread(2)
    gather(0)
    multiply(1)
    gather(1)
    multiply(2)
    gather(2)


def sample_kernel(
    r_ref, w_ref, cell_ref, table_ref, sum_ref, v_ref, g_ref, f_ref, tw_ref
):
    tw_ref[...] = twiddles(table_ref)
    for part in range(2):
        for group in range(12):
            piece = r_ref[pl.ds(part * 12 + group, 128, 24), :]
            v_ref[group * 128 : (group + 1) * 128, part * 128 : (part + 1) * 128] = piece.T
    for chunk in range(2):
        rows = slice(chunk * 768, (chunk + 1) * 768)
        v_high, v_low = halves(v_ref[rows, :])
        g_ref[rows, :] = (
            dot(v_high, table_ref[0:256, :])
            + dot(v_low, table_ref[0:256, :])
            + dot(v_high, table_ref[256:512, :])
        )

    def one_row(row):
        for t in range(3):
            base = (((row // 2) * 3 + t) * 2 + row % 2) * 64
            values = []
            for k1 in range(8):
                rows = pl.ds(pl.multiple_of(base + k1 * 8, 8), 8)
                value = (g_ref[rows, 0:128], g_ref[rows, 128:256])
                if k1 > 0:
                    twiddle = (
                        tw_ref[0 + k1 * 8 : 8 + k1 * 8, :],
                        tw_ref[64 + k1 * 8 : 72 + k1 * 8, :],
                    )
                    value = cmul_conj(value, twiddle)
                values.append(value)
            values = dft8(values, 1.0)
            for n1 in range(8):
                start = (row * 4 + n1 // 2) * CHAN + t * 8
                lanes = slice((n1 % 2) * 128, (n1 % 2) * 128 + 128)
                v_ref[pl.ds(pl.multiple_of(start, 8), 8), lanes] = values[n1][0]
                v_ref[pl.ds(pl.multiple_of(start + HALF, 8), 8), lanes] = values[n1][1]

    for row in range(8):
        one_row(row)
    f_high, f_low = halves(v_ref[...])
    f_ref[0] = f_high
    f_ref[1] = f_low
    place = lax.broadcasted_iota(jnp.int32, (256, 256), 0)
    for chunk in range(8):
        lanes = slice(chunk * 256, (chunk + 1) * 256)
        cells = cell_ref[:, lanes]
        hot = jnp.where(place == (cells & 255), 1.0, 0.0).astype(BF16)
        upper = cells >> 8
        total = jnp.zeros((CHAN, 256), F32)
        for quarter in range(4):
            rows = slice(quarter * 384, (quarter + 1) * 384)
            picked = dot(f_ref[0, rows, :], hot) + dot(f_ref[1, rows, :], hot)
            for part in range(8):
                hit = jnp.broadcast_to(upper == quarter * 8 + part, (CHAN, 256))
                total = total + jnp.where(hit, picked[part * CHAN : (part + 1) * CHAN, :], 0.0)
        sum_ref[:, lanes] = total * w_ref[:, lanes]

def finish_kernel(far_ref, near_ref, both_ref, side_ref, four_ref, out_ref, sum_ref):
    sum_ref[...] = far_ref[...] + near_ref[...]
    for cluster in range(4):
        lanes = slice(cluster * 4 * PIL, (cluster * 4 + 1) * PIL)
        sum_ref[:, lanes] += both_ref[:, cluster * PIL : (cluster + 1) * PIL].astype(F32)
        lanes = slice(cluster * PIL, (cluster + 1) * PIL)
        sum_ref[:, lanes] += both_ref[:, (cluster + 4) * PIL : (cluster + 5) * PIL].astype(F32)
    sum_ref[:, 3 * PIL : 4 * PIL] += side_ref[:, 4 * PIL : 5 * PIL].astype(F32)
    sum_ref[:, 15 * PIL : 16 * PIL] += four_ref[...].astype(F32)
    for slab in range(12):
        out_ref[slab] = sum_ref[slab * 4 : slab * 4 + 4, :]


def taylor(count, first):
    return [(-1.0) ** n / math.factorial(2 * n + first) for n in range(count)]


def horner(coefficients, square):
    total = jnp.full_like(square, coefficients[-1])
    for coefficient in coefficients[-2::-1]:
        total = total * square + coefficient
    return total


def near_kernel(
    list_ref, own_ref, both_ref, side_ref, four_ref, mix_ref,
    near_ref, back_one, back_side, back_four, all_ref, pos_ref, sum_ref,
):
    start = 0
    for data in (own_ref[...], both_ref[...], side_ref[:, 3 * PIL : 4 * PIL], four_ref[...]):
        width = data.shape[1]
        all_ref[:, start : start + width] = data[0:CHAN, :]
        pos_ref[:, start : start + width] = data[CHAN : CHAN + 16, :].astype(F32)
        start += width
    sum_ref[...] = jnp.zeros_like(sum_ref)
    wide_pos = list_ref[24]
    narrow_pos = list_ref[25]
    used = list_ref[26]
    local = lax.broadcasted_iota(jnp.int32, (1, PIL), 1)

    def place(wide, narrow, cluster, window):
        across = ((wide * CCX + cluster // CCY) * PCX + local // PCY).astype(F32)
        along = ((narrow * CCY + cluster % CCY) * PCY + local % PCY).astype(F32)
        return across * PITCH + pos_ref[0:1, window], along * PITCH + pos_ref[1:2, window]

    def column(vector):
        return jnp.broadcast_to(vector, (PIL, PIL)).T

    def mixed(values):
        return dot(mix_ref[...], values).astype(BF16)

    def one_slot(slot):
        direction = list_ref[slot * 3]
        own = list_ref[slot * 3 + 1]
        far = list_ref[slot * 3 + 2]
        move_wide = jnp.where(direction == 4, -1, jnp.where(direction >= 2, 1, 0))
        move_narrow = jnp.where(direction == 1, 1, jnp.where(direction >= 3, -1, 0))
        index = jnp.where(direction == 1, 16 + far // 4, far)
        index = jnp.where(direction == 2, 20 + far, index)
        index = jnp.where(direction == 3, 24, index)
        index = jnp.where(direction == 4, 25, index)
        own_window = pl.ds(pl.multiple_of(own * PIL, PIL), PIL)
        far_window = pl.ds(pl.multiple_of(index * PIL, PIL), PIL)
        own_x, own_y = place(wide_pos, narrow_pos, own, own_window)
        far_x, far_y = place(wide_pos + move_wide, narrow_pos + move_narrow, far, far_window)
        delta_x = column(own_x) - far_x
        delta_y = column(own_y) - far_y
        square = delta_x * delta_x + delta_y * delta_y
        over = lax.rsqrt(square)
        distance = square * over
        half_turns = (distance - jnp.round(distance)) * math.pi
        half_square = half_turns * half_turns
        half_sine = horner(taylor(7, 1), half_square) * half_turns
        half_cosine = horner(taylor(8, 0), half_square)
        cosine = 1.0 - 2.0 * half_sine * half_sine
        sine = 2.0 * half_sine * half_cosine
        unit_x = delta_x * over
        unit_y = delta_y * over
        inverse = over * (1.0 / (2.0 * math.pi))
        inverse_square = inverse * inverse
        green = (cosine * inverse, sine * inverse)
        term_a = cmul(green, (1.0 - inverse_square, inverse))
        term_b = cmul(green, (3.0 * inverse_square - 1.0, -3.0 * inverse))
        term_c = (green[0] - green[1] * inverse, green[1] + green[0] * inverse)
        unit_xx = unit_x * unit_x
        unit_xy = unit_x * unit_y
        unit_yy = unit_y * unit_y
        own_mixed = mixed(all_ref[:, own_window])
        far_mixed = mixed(all_ref[:, far_window])
        fields = []
        for field in range(6):
            for part in range(2):
                value = (
                    term_a[part],
                    term_b[part] * unit_xx,
                    term_b[part] * unit_xy,
                    term_b[part] * unit_yy,
                    term_c[part] * unit_x,
                    term_c[part] * unit_y,
                )[field].astype(BF16)
                fields.append(value)
        far_wide = jnp.concatenate([far_mixed[k * CHAN : (k + 1) * CHAN] for k in range(12)], axis=1)
        own_wide = jnp.concatenate([own_mixed[k * CHAN : (k + 1) * CHAN] for k in range(12)], axis=1)
        to_own = dot(far_wide, jnp.concatenate(fields, axis=1), 1, 1)
        to_far = dot(own_wide, jnp.concatenate(fields, axis=0), 1, 0)
        active = jnp.where(slot < used, 1.0, 0.0)
        return own_window, far_window, to_own * active, to_far * active

    def some_slots(step, carry):
        results = [one_slot(step * 4 + place) for place in range(4)]
        for own_window, far_window, to_own, to_far in results:
            sum_ref[:, own_window] += to_own
            sum_ref[:, far_window] += to_far
        return carry

    lax.fori_loop(0, (used + 3) // 4, some_slots, 0)
    near_ref[...] = sum_ref[:, 0:WIDTH]
    start = WIDTH
    for back in (back_one, back_side, back_four):
        width = back.shape[1]
        back[...] = sum_ref[:, start : start + width].astype(BF16)
        start += width


def shape(dims, kind=F32):
    return jax.ShapeDtypeStruct(dims, kind)


def shift(value, move_wide, move_narrow):
    pairs = []
    for wide in range(N_WIDE):
        for narrow in range(N_NARROW):
            to_wide, to_narrow = wide + move_wide, (narrow + move_narrow) % N_NARROW
            if 0 <= to_wide < N_WIDE:
                pairs.append((wide * N_NARROW + narrow, to_wide * N_NARROW + to_narrow))
    return lax.ppermute(value, AXES, pairs)


PARAMS = pltpu.CompilerParams(vmem_limit_bytes=48 * MIB)


def cost(flops, size):
    return pl.CostEstimate(flops=flops, bytes_accessed=size, transcendentals=0)


def pack_call(x, jitter):
    return pl.pallas_call(
        pack_kernel,
        out_shape=[
            shape((64, WIDTH), BF16),
            shape((64, 4 * PIL), BF16),
            shape((64, 4 * PIL), BF16),
            shape((64, PIL), BF16),
        ],
        scratch_shapes=[pltpu.VMEM((64, WIDTH), F32)],
        compiler_params=PARAMS,
        cost_estimate=cost(1_000_000, MIB // 2),
    )(x, jitter)


def rows_call(x, w, cell, table):
    return pl.pallas_call(
        rows_kernel,
        out_shape=shape((DEVICES * HALF, 128)),
        scratch_shapes=[
            pltpu.VMEM((CHAN, WIDTH), F32),
            pltpu.VMEM((CHAN, WIDTH), BF16),
            pltpu.VMEM((1536, WIDTH), BF16),
            pltpu.VMEM((2, 256, WIDTH), BF16),
            pltpu.VMEM((1536, 256), F32),
            pltpu.VMEM((1536, 256), F32),
            pltpu.VMEM((128, 128), F32),
        ],
        compiler_params=PARAMS,
        cost_estimate=cost(3_800_000_000, 4 * MIB),
    )(x, w, cell, table)


def near_call(spots, own, both, side, four, mixing):
    return pl.pallas_call(
        near_kernel,
        in_specs=[pl.BlockSpec(memory_space=pltpu.SMEM)] + [pl.BlockSpec(memory_space=pltpu.VMEM)] * 5,
        out_shape=[
            shape((CHAN, WIDTH)),
            shape((CHAN, 4 * PIL), BF16),
            shape((CHAN, 5 * PIL), BF16),
            shape((CHAN, PIL), BF16),
        ],
        scratch_shapes=[
            pltpu.VMEM((CHAN, WIDTH + HALO * PIL), BF16),
            pltpu.VMEM((16, WIDTH + HALO * PIL), F32),
            pltpu.VMEM((CHAN, WIDTH + HALO * PIL), F32),
        ],
        compiler_params=PARAMS,
        cost_estimate=cost(8_000_000_000, 4 * MIB),
    )(spots, own, both, side, four, mixing)


def columns_call(columns, transfer, forward, backward, column_table, lane_table):
    return pl.pallas_call(
        columns_kernel,
        out_shape=shape((DEVICES * HALF, 128)),
        scratch_shapes=[pltpu.VMEM((256, 1536), F32)] * 3,
        compiler_params=PARAMS,
        cost_estimate=cost(2_000_000_000, 6 * MIB),
    )(columns, transfer, forward, backward, column_table, lane_table)


def sample_call(rows, w, cell, table):
    return pl.pallas_call(
        sample_kernel,
        out_shape=shape((CHAN, WIDTH)),
        scratch_shapes=[
            pltpu.VMEM((1536, 256), F32),
            pltpu.VMEM((1536, 256), F32),
            pltpu.VMEM((2, 1536, 256), BF16),
            pltpu.VMEM((128, 128), F32),
        ],
        compiler_params=PARAMS,
        cost_estimate=cost(3_800_000_000, 4 * MIB),
    )(rows, w, cell, table)


def finish_call(far, near, both, side, four):
    return pl.pallas_call(
        finish_kernel,
        out_shape=shape((12, 4, WIDTH)),
        scratch_shapes=[pltpu.VMEM((CHAN, WIDTH), F32)],
        compiler_params=PARAMS,
        cost_estimate=cost(1_000_000, 2 * MIB),
    )(far, near, both, side, four)


def exchange(message):
    code = message.reshape(DEVICES, HALF, 128).astype(jnp.float16)
    code = lax.all_to_all(code, AXES, split_axis=0, concat_axis=0, tiled=True)
    code = code.astype(F32)
    return (code * jnp.abs(code)).reshape(DEVICES * HALF, 128)


def local(incident, jitter, weights, cells, pair_list, pair_count, kernel):
    x = incident.transpose(0, 2, 1, 3).reshape(12, ANG, WIDTH)
    w = weights.reshape(1, WIDTH)
    cell = cells.reshape(1, WIDTH)
    forward = jnp.asarray(dft_table(-1.0))
    table = jnp.asarray(row_table())

    message = rows_call(x, w, cell, table)
    columns = exchange(message)
    own, one, two, four = pack_call(x, jitter)
    side = shift(two, -1, 1)
    four = shift(four, 1, 1)
    both = shift(jnp.concatenate([one, side], axis=1), 0, -1)

    transfer = kernel.reshape(2, 2, 4, 128, 8).transpose(0, 2, 3, 1, 4)
    transfer = jnp.broadcast_to(transfer[..., None], (2, 4, 128, 2, 8, 8)).reshape(2, 512, 128)
    message = columns_call(
        columns,
        transfer,
        forward,
        jnp.asarray(dft_table(1.0, 1.0 / 1048576)),
        jnp.asarray(column_twiddle()),
        jnp.asarray(lane_twiddle()),
    )
    rows = exchange(message)

    spots = jnp.concatenate(
        [
            pair_list.reshape(PAIRS * 3),
            lax.axis_index("wide").reshape(1),
            lax.axis_index("narrow").reshape(1),
            pair_count,
        ]
    )
    near, one, side, four = near_call(spots, own, both, side, four, jnp.asarray(mixing_table()))
    side = shift(side, 1, -1)
    four = shift(four, -1, -1)
    both = shift(jnp.concatenate([one, side[:, 0 : 4 * PIL]], axis=1), 0, 1)
    far = sample_call(rows, w, cell, table)
    coupled = finish_call(far, near, both, side, four)
    return coupled.reshape(2, 6, ANG, WIDTH).transpose(0, 2, 1, 3)


def solution(mesh):
    in_specs = (
        P(None, None, None, AXES),
        P(None, AXES),
        P(AXES),
        P(AXES),
        P(AXES, None, None),
        P(AXES),
        P(None, None, AXES),
    )
    return jax.shard_map(
        local, mesh=mesh, in_specs=in_specs, out_specs=P(None, None, None, AXES), check_vma=False
    )
```

```python
import math

import jax
import jax.numpy as jnp
import numpy as np
from jax import lax
from jax.experimental import pallas as pl
from jax.experimental.pallas import tpu as pltpu
from jax.sharding import PartitionSpec as P

ANG = 4
PCX = 8
PCY = 16
CCX = 4
CCY = 4
PIL = 128
CHAN = 48
HALF = 24
WIDTH = 2048
PAIRS = 8
N_WIDE = 16
N_NARROW = 8
DEVICES = 128
AXES = ("wide", "narrow")
PITCH = 0.4
BF16 = jnp.bfloat16
F32 = jnp.float32
HALO = 10
MIB = 1 << 20


def split_table(table):
    high = table.astype(BF16)
    low = (table - high.astype(np.float64)).astype(BF16)
    return np.stack([high, low])


def dft_table(sign, scale=1.0):
    ids = np.arange(128)
    angles = (ids[:, None] * ids[None, :] % 128) * (2.0 * math.pi / 128)
    cosine = np.cos(angles) * scale
    sine = np.sin(angles) * scale * sign
    return split_table(np.block([[cosine, -sine], [sine, cosine]]))


def row_table():
    k1 = np.repeat(np.arange(8), 8)
    angles = (k1[:, None] * np.arange(128)[None, :]) * (2.0 * math.pi / 1024)
    twiddle = split_table(np.concatenate([np.cos(angles), -np.sin(angles)]))
    return np.concatenate([*dft_table(-1.0), np.concatenate([*twiddle], axis=1)])


def column_twiddle():
    row = (np.arange(128) // 64)[None, None, :] + 2 * np.arange(4)[:, None, None]
    angles = (row * np.arange(128)[None, :, None]) * (2.0 * math.pi / 1024)
    return np.stack([np.cos(angles), -np.sin(angles)]).reshape(2, 512, 128).astype(np.float32)


def lane_twiddle():
    side = (np.arange(128) // 64)[None, :]
    angles = np.arange(4)[:, None] * side * (2.0 * math.pi / 8)
    table = np.concatenate([np.cos(angles), -np.sin(angles), np.where(side == 0, 1.0, -1.0)])
    return np.concatenate([table, np.zeros((7, 128))]).astype(np.float32)


def mixing_table():
    table = np.zeros((6, 6, 6), np.float32)
    for member in range(6):
        table[0, member, member] = 1.0
    for offset in (0, 3):
        table[1, offset, offset] = 1.0
        table[2, offset, offset + 1] = 1.0
        table[2, offset + 1, offset] = 1.0
        table[3, offset + 1, offset + 1] = 1.0
    table[4, 2, 4] = 1.0
    table[4, 4, 2] = 1.0
    table[4, 1, 5] = -1.0
    table[4, 5, 1] = -1.0
    table[5, 0, 5] = 1.0
    table[5, 5, 0] = 1.0
    table[5, 2, 3] = -1.0
    table[5, 3, 2] = -1.0
    parts = np.zeros((2, 2, 2), np.float32)
    parts[0] = np.eye(2)
    parts[1] = np.array([[0.0, -1.0], [1.0, 0.0]])
    full = np.einsum("fab,rop,gh->froagpbh", table, parts, np.eye(ANG))
    return full.reshape(12 * CHAN, CHAN).astype(BF16)


def dot(left, right, left_dim=1, right_dim=0):
    return lax.dot_general(
        left, right, (((left_dim,), (right_dim,)), ((), ())), preferred_element_type=F32
    )


def halves(value):
    high = value.astype(BF16)
    return high, (value - high.astype(F32)).astype(BF16)


STEP = 585.0
FLOOR = 36.0


def coded(value):
    size = jnp.log(jnp.maximum(jnp.abs(value), 2.0**-FLOOR))
    code = size * (STEP / math.log(2.0)) + (FLOOR * STEP + 0.5)
    return (code * jnp.clip(value * 2.0**60, -1.0, 1.0)).astype(jnp.int32)


def decoded(code):
    code = code.astype(F32)
    return jnp.exp2(jnp.abs(code) * (1.0 / STEP) - FLOOR) * jnp.clip(code, -1.0, 1.0)


def rooted(value):
    return value * lax.rsqrt(jnp.maximum(jnp.abs(value), 1e-30))


def cadd(left, right):
    return (left[0] + right[0], left[1] + right[1])


def csub(left, right):
    return (left[0] - right[0], left[1] - right[1])


def cmul(left, right):
    return (left[0] * right[0] - left[1] * right[1], left[0] * right[1] + left[1] * right[0])


def cmul_conj(left, right):
    return (left[0] * right[0] + left[1] * right[1], left[1] * right[0] - left[0] * right[1])


def turn(value, sign):
    if sign < 0:
        return (value[1], -value[0])
    return (-value[1], value[0])


def dft4(values, sign):
    even, odd = cadd(values[0], values[2]), csub(values[0], values[2])
    left, right = cadd(values[1], values[3]), turn(csub(values[1], values[3]), sign)
    return [cadd(even, left), cadd(odd, right), csub(even, left), csub(odd, right)]


def dft8(values, sign):
    even = dft4(values[0::2], sign)
    odd = dft4(values[1::2], sign)
    root = math.sqrt(0.5)
    first, third = odd[1], odd[3]
    odd[1] = ((first[0] - sign * first[1]) * root, (first[1] + sign * first[0]) * root)
    odd[2] = turn(odd[2], sign)
    odd[3] = ((-third[0] - sign * third[1]) * root, (-third[1] + sign * third[0]) * root)
    return [cadd(e, o) for e, o in zip(even, odd)] + [csub(e, o) for e, o in zip(even, odd)]


def pack_kernel(x_ref, jitter_ref, own_ref, one_ref, two_ref, four_ref, pack_ref):
    for slab in range(12):
        pack_ref[slab * 4 : slab * 4 + 4, :] = x_ref[slab].astype(F32)
    pack_ref[CHAN : CHAN + 16, :] = jnp.zeros((16, WIDTH), F32)
    pack_ref[CHAN : CHAN + 2, :] = jitter_ref[...].astype(F32)
    own_ref[...] = pack_ref[...].astype(BF16)
    for cluster in range(4):
        one_ref[:, cluster * PIL : (cluster + 1) * PIL] = own_ref[:, cluster * 4 * PIL : (cluster * 4 + 1) * PIL]
    two_ref[...] = own_ref[:, 0 : 4 * PIL]
    four_ref[...] = own_ref[:, 15 * PIL : 16 * PIL]


def twiddles(table_ref):
    return table_ref[512:640, 0:128].astype(F32) + table_ref[512:640, 128:256].astype(F32)


def rows_kernel(
    x_hbm, w_hbm, cell_hbm, table_hbm, out_ref,
    x_ref, w_ref, cell_ref, table_ref, pack_ref, xb_ref, xt_ref, hot_ref, g_ref, b_ref, tw_ref, code_ref, sems,
):
    pairs = ((cell_hbm, cell_ref), (w_hbm, w_ref), (x_hbm, x_ref), (table_hbm, table_ref))
    copies = [
        pltpu.make_async_copy(source, target, sems.at[place])
        for place, (source, target) in enumerate(pairs)
    ]
    for copy in copies:
        copy.start()
    copies[0].wait()
    copies[1].wait()
    cells = cell_ref[...]
    upper = cells >> 8
    weight = w_ref[...]
    high = weight.astype(BF16).astype(F32)
    low = weight - high
    for block in range(16):
        place = lax.broadcasted_iota(jnp.int32, (16, WIDTH), 0) + block * 16
        hit = place == (cells & 255)
        hot_ref[0, block * 16 : block * 16 + 16, :] = jnp.where(hit, high, 0.0).astype(BF16)
        hot_ref[1, block * 16 : block * 16 + 16, :] = jnp.where(hit, low, 0.0).astype(BF16)
    copies[2].wait()
    for slab in range(12):
        pack_ref[slab * 4 : slab * 4 + 4, :] = x_ref[slab].astype(F32)
    xb_ref[...] = pack_ref[...].astype(BF16)
    for part in range(32):
        mask = jnp.where(upper == part, 1.0, 0.0).astype(BF16)
        xt_ref[part * CHAN : (part + 1) * CHAN, :] = xb_ref[...] * mask
    for chunk in range(2):
        rows = slice(chunk * 768, (chunk + 1) * 768)
        piece = xt_ref[rows, :]
        g_ref[rows, :] = dot(piece, hot_ref[0], 1, 1) + dot(piece, hot_ref[1], 1, 1)

    copies[3].wait()
    tw_ref[...] = twiddles(table_ref)

    def one_row(row):
        for t in range(3):
            values = []
            for n1 in range(8):
                start = (row * 4 + n1 // 2) * CHAN + t * 8
                lanes = slice((n1 % 2) * 128, (n1 % 2) * 128 + 128)
                values.append(
                    (
                        g_ref[pl.ds(pl.multiple_of(start, 8), 8), lanes],
                        g_ref[pl.ds(pl.multiple_of(start + HALF, 8), 8), lanes],
                    )
                )
            values = dft8(values, -1.0)
            base = (((row // 2) * 3 + t) * 2 + row % 2) * 64
            for k1 in range(8):
                value = values[k1]
                if k1 > 0:
                    twiddle = (
                        tw_ref[0 + k1 * 8 : 8 + k1 * 8, :],
                        tw_ref[64 + k1 * 8 : 72 + k1 * 8, :],
                    )
                    value = cmul(value, twiddle)
                rows = pl.ds(pl.multiple_of(base + k1 * 8, 8), 8)
                b_ref[rows, 0:128] = value[0]
                b_ref[rows, 128:256] = value[1]

    for row in range(8):
        one_row(row)
    for pair in range(6):
        b_high, b_low = halves(b_ref[pair * 256 : (pair + 1) * 256, :])
        result = (
            dot(table_ref[0:256, :], b_high, 1, 1)
            + dot(table_ref[0:256, :], b_low, 1, 1)
            + dot(table_ref[256:512, :], b_high, 1, 1)
        )
        result = coded(result)
        for part in range(2):
            for side in range(2):
                code_ref[pl.ds(part * 12 + pair * 2 + side, 128, 24), :] = result[
                    part * 128 : (part + 1) * 128, side * 128 : (side + 1) * 128
                ]
    out_ref[...] = code_ref[...].astype(jnp.int16)


def columns_kernel(
    r_ref, kern_ref, fwd_ref, inv_ref, tw_ref, lane_ref, out_ref, v_ref, u_ref, y_ref, code_ref
):
    code_ref[...] = r_ref[...].astype(jnp.int32)
    sign = lane_ref[8:9, :]

    def swap(value):
        return tuple(part * sign + pltpu.roll(part, 64, 1) for part in value)

    def lanes_of(t, m):
        return slice((t * 4 + m) * 128, (t * 4 + m + 1) * 128)

    def spread(t):
        for part in range(2):
            for m in range(4):
                v_ref[part * 128 : (part + 1) * 128, lanes_of(t, m)] = decoded(
                    code_ref[pl.ds(part * 12 + m * 3 + t, 128, 24), :]
                )
        for chunk in range(2):
            lanes = slice((t * 2 + chunk) * 256, (t * 2 + chunk + 1) * 256)
            v_high, v_low = halves(v_ref[:, lanes])
            u_ref[:, lanes] = dot(fwd_ref[0], v_high) + dot(fwd_ref[0], v_low) + dot(fwd_ref[1], v_high)

    def multiply(t):
        for block in range(16):
            re_rows = slice(block * 8, block * 8 + 8)
            im_rows = slice(block * 8 + 128, block * 8 + 136)
            values, twiddles = [], []
            for m in range(4):
                rows = slice(m * 128 + block * 8, m * 128 + block * 8 + 8)
                twiddles.append((tw_ref[0, rows, :], tw_ref[1, rows, :]))
                lanes = lanes_of(t, m)
                values.append(cmul((u_ref[re_rows, lanes], u_ref[im_rows, lanes]), twiddles[m]))
            values = dft4(values, -1.0)
            for a in range(4):
                rows = slice(a * 128 + block * 8, a * 128 + block * 8 + 8)
                side = (lane_ref[a : a + 1, :], lane_ref[4 + a : 5 + a, :])
                value = values[a] if a == 0 else cmul(values[a], side)
                value = swap(cmul(swap(value), (kern_ref[0, rows, :], kern_ref[1, rows, :])))
                values[a] = value if a == 0 else cmul_conj(value, side)
            values = dft4(values, 1.0)
            for m in range(4):
                value = cmul_conj(values[m], twiddles[m])
                y_ref[re_rows, lanes_of(t, m)] = value[0]
                y_ref[im_rows, lanes_of(t, m)] = value[1]

    def gather(t):
        for chunk in range(2):
            lanes = slice((t * 2 + chunk) * 256, (t * 2 + chunk + 1) * 256)
            y_high, y_low = halves(y_ref[:, lanes])
            result = rooted(dot(inv_ref[0], y_high) + dot(inv_ref[0], y_low) + dot(inv_ref[1], y_high))
            for part in range(2):
                for side in range(2):
                    out_ref[pl.ds(part * 12 + (chunk * 2 + side) * 3 + t, 128, 24), :] = result[
                        part * 128 : (part + 1) * 128, side * 128 : (side + 1) * 128
                    ]

    spread(0)
    spread(1)
    multiply(0)
    spread(2)
    gather(0)
    multiply(1)
    gather(1)
    multiply(2)
    gather(2)


def sample_kernel(
    r_ref, w_ref, cell_ref, table_ref, sum_ref, v_ref, g_ref, f_ref, tw_ref
):
    tw_ref[...] = twiddles(table_ref)
    for part in range(2):
        for group in range(12):
            piece = r_ref[pl.ds(part * 12 + group, 128, 24), :]
            v_ref[group * 128 : (group + 1) * 128, part * 128 : (part + 1) * 128] = piece.T
    for chunk in range(2):
        rows = slice(chunk * 768, (chunk + 1) * 768)
        v_high, v_low = halves(v_ref[rows, :])
        g_ref[rows, :] = (
            dot(v_high, table_ref[0:256, :])
            + dot(v_low, table_ref[0:256, :])
            + dot(v_high, table_ref[256:512, :])
        )

    def one_row(row):
        for t in range(3):
            base = (((row // 2) * 3 + t) * 2 + row % 2) * 64
            values = []
            for k1 in range(8):
                rows = pl.ds(pl.multiple_of(base + k1 * 8, 8), 8)
                value = (g_ref[rows, 0:128], g_ref[rows, 128:256])
                if k1 > 0:
                    twiddle = (
                        tw_ref[0 + k1 * 8 : 8 + k1 * 8, :],
                        tw_ref[64 + k1 * 8 : 72 + k1 * 8, :],
                    )
                    value = cmul_conj(value, twiddle)
                values.append(value)
            values = dft8(values, 1.0)
            for n1 in range(8):
                start = (row * 4 + n1 // 2) * CHAN + t * 8
                lanes = slice((n1 % 2) * 128, (n1 % 2) * 128 + 128)
                v_ref[pl.ds(pl.multiple_of(start, 8), 8), lanes] = values[n1][0]
                v_ref[pl.ds(pl.multiple_of(start + HALF, 8), 8), lanes] = values[n1][1]

    for row in range(8):
        one_row(row)
    f_high, f_low = halves(v_ref[...])
    f_ref[0] = f_high
    f_ref[1] = f_low
    place = lax.broadcasted_iota(jnp.int32, (256, 256), 0)
    for chunk in range(8):
        lanes = slice(chunk * 256, (chunk + 1) * 256)
        cells = cell_ref[:, lanes]
        hot = jnp.where(place == (cells & 255), 1.0, 0.0).astype(BF16)
        upper = cells >> 8
        total = jnp.zeros((CHAN, 256), F32)
        for quarter in range(4):
            rows = slice(quarter * 384, (quarter + 1) * 384)
            picked = dot(f_ref[0, rows, :], hot) + dot(f_ref[1, rows, :], hot)
            for part in range(8):
                hit = jnp.broadcast_to(upper == quarter * 8 + part, (CHAN, 256))
                total = total + jnp.where(hit, picked[part * CHAN : (part + 1) * CHAN, :], 0.0)
        sum_ref[:, lanes] = total * w_ref[:, lanes]

def finish_kernel(far_ref, near_ref, both_ref, side_ref, four_ref, out_ref, sum_ref):
    sum_ref[...] = far_ref[...] + near_ref[...]
    for cluster in range(4):
        lanes = slice(cluster * 4 * PIL, (cluster * 4 + 1) * PIL)
        sum_ref[:, lanes] += both_ref[:, cluster * PIL : (cluster + 1) * PIL].astype(F32)
        lanes = slice(cluster * PIL, (cluster + 1) * PIL)
        sum_ref[:, lanes] += both_ref[:, (cluster + 4) * PIL : (cluster + 5) * PIL].astype(F32)
    sum_ref[:, 3 * PIL : 4 * PIL] += side_ref[:, 4 * PIL : 5 * PIL].astype(F32)
    sum_ref[:, 15 * PIL : 16 * PIL] += four_ref[...].astype(F32)
    for slab in range(12):
        out_ref[slab] = sum_ref[slab * 4 : slab * 4 + 4, :]


def taylor(count, first):
    return [(-1.0) ** n / math.factorial(2 * n + first) for n in range(count)]


def horner(coefficients, square):
    total = jnp.full_like(square, coefficients[-1])
    for coefficient in coefficients[-2::-1]:
        total = total * square + coefficient
    return total


def near_kernel(
    list_ref, own_ref, both_ref, side_ref, four_ref, mix_ref,
    near_ref, back_one, back_side, back_four, all_ref, pos_ref, sum_ref,
):
    start = 0
    for data in (own_ref[...], both_ref[...], side_ref[:, 3 * PIL : 4 * PIL], four_ref[...]):
        width = data.shape[1]
        all_ref[:, start : start + width] = data[0:CHAN, :]
        pos_ref[:, start : start + width] = data[CHAN : CHAN + 16, :].astype(F32)
        start += width
    sum_ref[...] = jnp.zeros_like(sum_ref)
    wide_pos = list_ref[24]
    narrow_pos = list_ref[25]
    used = list_ref[26]
    local = lax.broadcasted_iota(jnp.int32, (1, PIL), 1)

    def place(wide, narrow, cluster, window):
        across = ((wide * CCX + cluster // CCY) * PCX + local // PCY).astype(F32)
        along = ((narrow * CCY + cluster % CCY) * PCY + local % PCY).astype(F32)
        return across * PITCH + pos_ref[0:1, window], along * PITCH + pos_ref[1:2, window]

    def column(vector):
        return jnp.broadcast_to(vector, (PIL, PIL)).T

    def mixed(values):
        return dot(mix_ref[...], values).astype(BF16)

    def one_slot(slot):
        direction = list_ref[slot * 3]
        own = list_ref[slot * 3 + 1]
        far = list_ref[slot * 3 + 2]
        move_wide = jnp.where(direction == 4, -1, jnp.where(direction >= 2, 1, 0))
        move_narrow = jnp.where(direction == 1, 1, jnp.where(direction >= 3, -1, 0))
        index = jnp.where(direction == 1, 16 + far // 4, far)
        index = jnp.where(direction == 2, 20 + far, index)
        index = jnp.where(direction == 3, 24, index)
        index = jnp.where(direction == 4, 25, index)
        own_window = pl.ds(pl.multiple_of(own * PIL, PIL), PIL)
        far_window = pl.ds(pl.multiple_of(index * PIL, PIL), PIL)
        own_x, own_y = place(wide_pos, narrow_pos, own, own_window)
        far_x, far_y = place(wide_pos + move_wide, narrow_pos + move_narrow, far, far_window)
        delta_x = column(own_x) - far_x
        delta_y = column(own_y) - far_y
        square = delta_x * delta_x + delta_y * delta_y
        over = lax.rsqrt(square)
        distance = square * over
        half_turns = (distance - jnp.round(distance)) * math.pi
        half_square = half_turns * half_turns
        half_sine = horner(taylor(7, 1), half_square) * half_turns
        half_cosine = horner(taylor(8, 0), half_square)
        cosine = 1.0 - 2.0 * half_sine * half_sine
        sine = 2.0 * half_sine * half_cosine
        unit_x = delta_x * over
        unit_y = delta_y * over
        inverse = over * (1.0 / (2.0 * math.pi))
        inverse_square = inverse * inverse
        green = (cosine * inverse, sine * inverse)
        term_a = cmul(green, (1.0 - inverse_square, inverse))
        term_b = cmul(green, (3.0 * inverse_square - 1.0, -3.0 * inverse))
        term_c = (green[0] - green[1] * inverse, green[1] + green[0] * inverse)
        unit_xx = unit_x * unit_x
        unit_xy = unit_x * unit_y
        unit_yy = unit_y * unit_y
        own_mixed = mixed(all_ref[:, own_window])
        far_mixed = mixed(all_ref[:, far_window])
        fields = []
        for field in range(6):
            for part in range(2):
                value = (
                    term_a[part],
                    term_b[part] * unit_xx,
                    term_b[part] * unit_xy,
                    term_b[part] * unit_yy,
                    term_c[part] * unit_x,
                    term_c[part] * unit_y,
                )[field].astype(BF16)
                fields.append(value)
        far_wide = jnp.concatenate([far_mixed[k * CHAN : (k + 1) * CHAN] for k in range(12)], axis=1)
        own_wide = jnp.concatenate([own_mixed[k * CHAN : (k + 1) * CHAN] for k in range(12)], axis=1)
        to_own = dot(far_wide, jnp.concatenate(fields, axis=1), 1, 1)
        to_far = dot(own_wide, jnp.concatenate(fields, axis=0), 1, 0)
        active = jnp.where(slot < used, 1.0, 0.0)
        return own_window, far_window, to_own * active, to_far * active

    def some_slots(step, carry):
        results = [one_slot(step * 4 + place) for place in range(4)]
        for own_window, far_window, to_own, to_far in results:
            sum_ref[:, own_window] += to_own
            sum_ref[:, far_window] += to_far
        return carry

    lax.fori_loop(0, (used + 3) // 4, some_slots, 0)
    near_ref[...] = sum_ref[:, 0:WIDTH]
    start = WIDTH
    for back in (back_one, back_side, back_four):
        width = back.shape[1]
        back[...] = sum_ref[:, start : start + width].astype(BF16)
        start += width


def shape(dims, kind=F32):
    return jax.ShapeDtypeStruct(dims, kind)


def shift(value, move_wide, move_narrow):
    pairs = []
    for wide in range(N_WIDE):
        for narrow in range(N_NARROW):
            to_wide, to_narrow = wide + move_wide, (narrow + move_narrow) % N_NARROW
            if 0 <= to_wide < N_WIDE:
                pairs.append((wide * N_NARROW + narrow, to_wide * N_NARROW + to_narrow))
    return lax.ppermute(value, AXES, pairs)


PARAMS = pltpu.CompilerParams(vmem_limit_bytes=48 * MIB)


def cost(flops, size):
    return pl.CostEstimate(flops=flops, bytes_accessed=size, transcendentals=0)


def pack_call(x, jitter):
    return pl.pallas_call(
        pack_kernel,
        out_shape=[
            shape((64, WIDTH), BF16),
            shape((64, 4 * PIL), BF16),
            shape((64, 4 * PIL), BF16),
            shape((64, PIL), BF16),
        ],
        scratch_shapes=[pltpu.VMEM((64, WIDTH), F32)],
        compiler_params=PARAMS,
        cost_estimate=cost(1_000_000, MIB // 2),
    )(x, jitter)


def rows_call(x, w, cell, table):
    return pl.pallas_call(
        rows_kernel,
        in_specs=[pl.BlockSpec(memory_space=pltpu.HBM)] * 4,
        out_shape=shape((DEVICES * HALF, 128), jnp.int16),
        scratch_shapes=[
            pltpu.VMEM((12, 4, WIDTH), BF16),
            pltpu.VMEM((1, WIDTH), F32),
            pltpu.VMEM((1, WIDTH), jnp.int32),
            pltpu.VMEM((640, 256), BF16),
            pltpu.VMEM((CHAN, WIDTH), F32),
            pltpu.VMEM((CHAN, WIDTH), BF16),
            pltpu.VMEM((1536, WIDTH), BF16),
            pltpu.VMEM((2, 256, WIDTH), BF16),
            pltpu.VMEM((1536, 256), F32),
            pltpu.VMEM((1536, 256), F32),
            pltpu.VMEM((128, 128), F32),
            pltpu.VMEM((DEVICES * HALF, 128), jnp.int32),
            pltpu.SemaphoreType.DMA((4,)),
        ],
        compiler_params=pltpu.CompilerParams(vmem_limit_bytes=63 * MIB),
        cost_estimate=cost(3_800_000_000, 4 * MIB),
    )(x, w, cell, table)


def near_call(spots, own, both, side, four, mixing):
    return pl.pallas_call(
        near_kernel,
        in_specs=[pl.BlockSpec(memory_space=pltpu.SMEM)] + [pl.BlockSpec(memory_space=pltpu.VMEM)] * 5,
        out_shape=[
            shape((CHAN, WIDTH)),
            shape((CHAN, 4 * PIL), BF16),
            shape((CHAN, 5 * PIL), BF16),
            shape((CHAN, PIL), BF16),
        ],
        scratch_shapes=[
            pltpu.VMEM((CHAN, WIDTH + HALO * PIL), BF16),
            pltpu.VMEM((16, WIDTH + HALO * PIL), F32),
            pltpu.VMEM((CHAN, WIDTH + HALO * PIL), F32),
        ],
        compiler_params=PARAMS,
        cost_estimate=cost(8_000_000_000, 4 * MIB),
    )(spots, own, both, side, four, mixing)


def columns_call(columns, transfer, forward, backward, column_table, lane_table):
    return pl.pallas_call(
        columns_kernel,
        out_shape=shape((DEVICES * HALF, 128)),
        scratch_shapes=[pltpu.VMEM((256, 1536), F32)] * 3 + [pltpu.VMEM((DEVICES * HALF, 128), jnp.int32)],
        compiler_params=PARAMS,
        cost_estimate=cost(2_000_000_000, 6 * MIB),
    )(columns, transfer, forward, backward, column_table, lane_table)


def sample_call(rows, w, cell, table):
    return pl.pallas_call(
        sample_kernel,
        out_shape=shape((CHAN, WIDTH)),
        scratch_shapes=[
            pltpu.VMEM((1536, 256), F32),
            pltpu.VMEM((1536, 256), F32),
            pltpu.VMEM((2, 1536, 256), BF16),
            pltpu.VMEM((128, 128), F32),
        ],
        compiler_params=PARAMS,
        cost_estimate=cost(3_800_000_000, 4 * MIB),
    )(rows, w, cell, table)


def finish_call(far, near, both, side, four):
    return pl.pallas_call(
        finish_kernel,
        out_shape=shape((12, 4, WIDTH)),
        scratch_shapes=[pltpu.VMEM((CHAN, WIDTH), F32)],
        compiler_params=PARAMS,
        cost_estimate=cost(1_000_000, 2 * MIB),
    )(far, near, both, side, four)


def exchange(message):
    message = message.reshape(DEVICES, HALF, 128)
    message = lax.all_to_all(message, AXES, split_axis=0, concat_axis=0, tiled=True)
    return message.reshape(DEVICES * HALF, 128)


def local(incident, jitter, weights, cells, pair_list, pair_count, kernel):
    x = incident.transpose(0, 2, 1, 3).reshape(12, ANG, WIDTH)
    w = weights.reshape(1, WIDTH)
    cell = cells.reshape(1, WIDTH)
    forward = jnp.asarray(dft_table(-1.0))
    table = jnp.asarray(row_table())

    message = rows_call(x, w, cell, table)
    columns = exchange(message)
    own, one, two, four = pack_call(x, jitter)
    side = shift(two, -1, 1)
    four = shift(four, 1, 1)
    both = shift(jnp.concatenate([one, side], axis=1), 0, -1)

    transfer = kernel.reshape(2, 2, 4, 128, 8).transpose(0, 2, 3, 1, 4)
    transfer = jnp.broadcast_to(transfer[..., None], (2, 4, 128, 2, 8, 8)).reshape(2, 512, 128)
    message = columns_call(
        columns,
        transfer,
        forward,
        jnp.asarray(dft_table(1.0, 1.0 / 1048576)),
        jnp.asarray(column_twiddle()),
        jnp.asarray(lane_twiddle()),
    )
    code = exchange(message.astype(jnp.float16)).astype(F32)
    rows = code * jnp.abs(code)

    spots = jnp.concatenate(
        [
            pair_list.reshape(PAIRS * 3),
            lax.axis_index("wide").reshape(1),
            lax.axis_index("narrow").reshape(1),
            pair_count,
        ]
    )
    near, one, side, four = near_call(spots, own, both, side, four, jnp.asarray(mixing_table()))
    side = shift(side, 1, -1)
    four = shift(four, -1, -1)
    both = shift(jnp.concatenate([one, side[:, 0 : 4 * PIL]], axis=1), 0, 1)
    far = sample_call(rows, w, cell, table)
    coupled = finish_call(far, near, both, side, four)
    return coupled.reshape(2, 6, ANG, WIDTH).transpose(0, 2, 1, 3)


def solution(mesh):
    in_specs = (
        P(None, None, None, AXES),
        P(None, AXES),
        P(AXES),
        P(AXES),
        P(AXES, None, None),
        P(AXES),
        P(None, None, AXES),
    )
    return jax.shard_map(
        local, mesh=mesh, in_specs=in_specs, out_specs=P(None, None, None, AXES), check_vma=False
    )
```

```python
import math

import jax
import jax.numpy as jnp
import numpy as np
from jax import lax
from jax.experimental import pallas as pl
from jax.experimental.pallas import tpu as pltpu
from jax.sharding import PartitionSpec as P

ANG = 4
PCX = 8
PCY = 16
CCX = 4
CCY = 4
PIL = 128
CHAN = 48
HALF = 24
WIDTH = 2048
PAIRS = 8
N_WIDE = 16
N_NARROW = 8
DEVICES = 128
AXES = ("wide", "narrow")
PITCH = 0.4
BF16 = jnp.bfloat16
F32 = jnp.float32
HALO = 10
MIB = 1 << 20


def split_table(table):
    high = table.astype(BF16)
    low = (table - high.astype(np.float64)).astype(BF16)
    return np.stack([high, low])


def dft_table(sign, scale=1.0):
    ids = np.arange(128)
    angles = (ids[:, None] * ids[None, :] % 128) * (2.0 * math.pi / 128)
    cosine = np.cos(angles) * scale
    sine = np.sin(angles) * scale * sign
    return split_table(np.block([[cosine, -sine], [sine, cosine]]))


def row_table():
    k1 = np.repeat(np.arange(8), 8)
    angles = (k1[:, None] * np.arange(128)[None, :]) * (2.0 * math.pi / 1024)
    twiddle = split_table(np.concatenate([np.cos(angles), -np.sin(angles)]))
    return np.concatenate([*dft_table(-1.0), np.concatenate([*twiddle], axis=1)])


def column_twiddle():
    row = (np.arange(128) // 64)[None, None, :] + 2 * np.arange(4)[:, None, None]
    angles = (row * np.arange(128)[None, :, None]) * (2.0 * math.pi / 1024)
    return np.stack([np.cos(angles), -np.sin(angles)]).reshape(2, 512, 128).astype(np.float32)


def lane_twiddle():
    side = (np.arange(128) // 64)[None, :]
    angles = np.arange(4)[:, None] * side * (2.0 * math.pi / 8)
    table = np.concatenate([np.cos(angles), -np.sin(angles), np.where(side == 0, 1.0, -1.0)])
    return np.concatenate([table, np.zeros((7, 128))]).astype(np.float32)


def mixing_table():
    table = np.zeros((6, 6, 6), np.float32)
    for member in range(6):
        table[0, member, member] = 1.0
    for offset in (0, 3):
        table[1, offset, offset] = 1.0
        table[2, offset, offset + 1] = 1.0
        table[2, offset + 1, offset] = 1.0
        table[3, offset + 1, offset + 1] = 1.0
    table[4, 2, 4] = 1.0
    table[4, 4, 2] = 1.0
    table[4, 1, 5] = -1.0
    table[4, 5, 1] = -1.0
    table[5, 0, 5] = 1.0
    table[5, 5, 0] = 1.0
    table[5, 2, 3] = -1.0
    table[5, 3, 2] = -1.0
    parts = np.zeros((2, 2, 2), np.float32)
    parts[0] = np.eye(2)
    parts[1] = np.array([[0.0, -1.0], [1.0, 0.0]])
    full = np.einsum("fab,rop,gh->froagpbh", table, parts, np.eye(ANG))
    return full.reshape(12 * CHAN, CHAN).astype(BF16)


def dot(left, right, left_dim=1, right_dim=0):
    return lax.dot_general(
        left, right, (((left_dim,), (right_dim,)), ((), ())), preferred_element_type=F32
    )


def halves(value):
    high = value.astype(BF16)
    return high, (value - high.astype(F32)).astype(BF16)


STEP = 585.0
FLOOR = 36.0


def coded(value):
    size = jnp.log(jnp.maximum(jnp.abs(value), 2.0**-FLOOR))
    code = size * (STEP / math.log(2.0)) + (FLOOR * STEP + 0.5)
    return (code * jnp.clip(value * 2.0**60, -1.0, 1.0)).astype(jnp.int32)


def decoded(code):
    code = code.astype(F32)
    return jnp.exp2(jnp.abs(code) * (1.0 / STEP) - FLOOR) * jnp.clip(code, -1.0, 1.0)


def packed(real, imag):
    return (coded(real) << 16) | (coded(imag) & 0xFFFF)


def unpacked(word):
    return decoded(word >> 16), decoded((word << 16) >> 16)


def cadd(left, right):
    return (left[0] + right[0], left[1] + right[1])


def csub(left, right):
    return (left[0] - right[0], left[1] - right[1])


def cmul(left, right):
    return (left[0] * right[0] - left[1] * right[1], left[0] * right[1] + left[1] * right[0])


def cmul_conj(left, right):
    return (left[0] * right[0] + left[1] * right[1], left[1] * right[0] - left[0] * right[1])


def turn(value, sign):
    if sign < 0:
        return (value[1], -value[0])
    return (-value[1], value[0])


def dft4(values, sign):
    even, odd = cadd(values[0], values[2]), csub(values[0], values[2])
    left, right = cadd(values[1], values[3]), turn(csub(values[1], values[3]), sign)
    return [cadd(even, left), cadd(odd, right), csub(even, left), csub(odd, right)]


def dft8(values, sign):
    even = dft4(values[0::2], sign)
    odd = dft4(values[1::2], sign)
    root = math.sqrt(0.5)
    first, third = odd[1], odd[3]
    odd[1] = ((first[0] - sign * first[1]) * root, (first[1] + sign * first[0]) * root)
    odd[2] = turn(odd[2], sign)
    odd[3] = ((-third[0] - sign * third[1]) * root, (-third[1] + sign * third[0]) * root)
    return [cadd(e, o) for e, o in zip(even, odd)] + [csub(e, o) for e, o in zip(even, odd)]


def pack_kernel(x_ref, jitter_ref, own_ref, one_ref, two_ref, four_ref, pack_ref):
    for slab in range(12):
        pack_ref[slab * 4 : slab * 4 + 4, :] = x_ref[slab].astype(F32)
    pack_ref[CHAN : CHAN + 16, :] = jnp.zeros((16, WIDTH), F32)
    pack_ref[CHAN : CHAN + 2, :] = jitter_ref[...].astype(F32)
    own_ref[...] = pack_ref[...].astype(BF16)
    for cluster in range(4):
        one_ref[:, cluster * PIL : (cluster + 1) * PIL] = own_ref[:, cluster * 4 * PIL : (cluster * 4 + 1) * PIL]
    two_ref[...] = own_ref[:, 0 : 4 * PIL]
    four_ref[...] = own_ref[:, 15 * PIL : 16 * PIL]


def twiddles(table_ref):
    return table_ref[512:640, 0:128].astype(F32) + table_ref[512:640, 128:256].astype(F32)


def rows_kernel(
    x_hbm, w_hbm, cell_hbm, table_hbm, out_ref,
    x_ref, w_ref, cell_ref, table_ref, pack_ref, xb_ref, xt_ref, hot_ref, g_ref, b_ref, tw_ref, sems,
):
    pairs = ((cell_hbm, cell_ref), (w_hbm, w_ref), (x_hbm, x_ref), (table_hbm, table_ref))
    copies = [
        pltpu.make_async_copy(source, target, sems.at[place])
        for place, (source, target) in enumerate(pairs)
    ]
    for copy in copies:
        copy.start()
    copies[0].wait()
    copies[1].wait()
    cells = cell_ref[...]
    upper = cells >> 8
    weight = w_ref[...]
    high = weight.astype(BF16).astype(F32)
    low = weight - high
    for block in range(16):
        place = lax.broadcasted_iota(jnp.int32, (16, WIDTH), 0) + block * 16
        hit = place == (cells & 255)
        hot_ref[0, block * 16 : block * 16 + 16, :] = jnp.where(hit, high, 0.0).astype(BF16)
        hot_ref[1, block * 16 : block * 16 + 16, :] = jnp.where(hit, low, 0.0).astype(BF16)
    copies[2].wait()
    for slab in range(12):
        pack_ref[slab * 4 : slab * 4 + 4, :] = x_ref[slab].astype(F32)
    xb_ref[...] = pack_ref[...].astype(BF16)
    for part in range(32):
        mask = jnp.where(upper == part, 1.0, 0.0).astype(BF16)
        xt_ref[part * CHAN : (part + 1) * CHAN, :] = xb_ref[...] * mask
    for chunk in range(2):
        rows = slice(chunk * 768, (chunk + 1) * 768)
        piece = xt_ref[rows, :]
        g_ref[rows, :] = dot(piece, hot_ref[0], 1, 1) + dot(piece, hot_ref[1], 1, 1)

    copies[3].wait()
    tw_ref[...] = twiddles(table_ref)

    def one_row(row):
        for t in range(3):
            values = []
            for n1 in range(8):
                start = (row * 4 + n1 // 2) * CHAN + t * 8
                lanes = slice((n1 % 2) * 128, (n1 % 2) * 128 + 128)
                values.append(
                    (
                        g_ref[pl.ds(pl.multiple_of(start, 8), 8), lanes],
                        g_ref[pl.ds(pl.multiple_of(start + HALF, 8), 8), lanes],
                    )
                )
            values = dft8(values, -1.0)
            base = (((row // 2) * 3 + t) * 2 + row % 2) * 64
            for k1 in range(8):
                value = values[k1]
                if k1 > 0:
                    twiddle = (
                        tw_ref[0 + k1 * 8 : 8 + k1 * 8, :],
                        tw_ref[64 + k1 * 8 : 72 + k1 * 8, :],
                    )
                    value = cmul(value, twiddle)
                rows = pl.ds(pl.multiple_of(base + k1 * 8, 8), 8)
                b_ref[rows, 0:128] = value[0]
                b_ref[rows, 128:256] = value[1]

    for row in range(8):
        one_row(row)
    for pair in range(6):
        b_high, b_low = halves(b_ref[pair * 256 : (pair + 1) * 256, :])
        result = (
            dot(table_ref[0:256, :], b_high, 1, 1)
            + dot(table_ref[0:256, :], b_low, 1, 1)
            + dot(table_ref[256:512, :], b_high, 1, 1)
        )
        for side in range(2):
            lanes = slice(side * 128, (side + 1) * 128)
            out_ref[pl.ds(pair * 2 + side, 128, 12), :] = packed(result[0:128, lanes], result[128:256, lanes])


def columns_kernel(r_ref, kern_ref, fwd_ref, inv_ref, tw_ref, lane_ref, out_ref, v_ref, u_ref, y_ref):
    sign = lane_ref[8:9, :]

    def swap(value):
        return tuple(part * sign + pltpu.roll(part, 64, 1) for part in value)

    def lanes_of(t, m):
        return slice((t * 4 + m) * 128, (t * 4 + m + 1) * 128)

    def spread(t):
        for m in range(4):
            real, imag = unpacked(r_ref[pl.ds(m * 3 + t, 128, 12), :])
            v_ref[0:128, lanes_of(t, m)] = real
            v_ref[128:256, lanes_of(t, m)] = imag
        for chunk in range(2):
            lanes = slice((t * 2 + chunk) * 256, (t * 2 + chunk + 1) * 256)
            v_high, v_low = halves(v_ref[:, lanes])
            u_ref[:, lanes] = dot(fwd_ref[0], v_high) + dot(fwd_ref[0], v_low) + dot(fwd_ref[1], v_high)

    def multiply(t):
        for block in range(16):
            re_rows = slice(block * 8, block * 8 + 8)
            im_rows = slice(block * 8 + 128, block * 8 + 136)
            values, twiddles = [], []
            for m in range(4):
                rows = slice(m * 128 + block * 8, m * 128 + block * 8 + 8)
                twiddles.append((tw_ref[0, rows, :], tw_ref[1, rows, :]))
                lanes = lanes_of(t, m)
                values.append(cmul((u_ref[re_rows, lanes], u_ref[im_rows, lanes]), twiddles[m]))
            values = dft4(values, -1.0)
            for a in range(4):
                rows = slice(a * 128 + block * 8, a * 128 + block * 8 + 8)
                side = (lane_ref[a : a + 1, :], lane_ref[4 + a : 5 + a, :])
                value = values[a] if a == 0 else cmul(values[a], side)
                value = swap(cmul(swap(value), (kern_ref[0, rows, :], kern_ref[1, rows, :])))
                values[a] = value if a == 0 else cmul_conj(value, side)
            values = dft4(values, 1.0)
            for m in range(4):
                value = cmul_conj(values[m], twiddles[m])
                y_ref[re_rows, lanes_of(t, m)] = value[0]
                y_ref[im_rows, lanes_of(t, m)] = value[1]

    def gather(t):
        for chunk in range(2):
            lanes = slice((t * 2 + chunk) * 256, (t * 2 + chunk + 1) * 256)
            y_high, y_low = halves(y_ref[:, lanes])
            result = dot(inv_ref[0], y_high) + dot(inv_ref[0], y_low) + dot(inv_ref[1], y_high)
            for side in range(2):
                lanes = slice(side * 128, (side + 1) * 128)
                out_ref[pl.ds((chunk * 2 + side) * 3 + t, 128, 12), :] = packed(
                    result[0:128, lanes], result[128:256, lanes]
                )

    spread(0)
    spread(1)
    multiply(0)
    spread(2)
    gather(0)
    multiply(1)
    gather(1)
    multiply(2)
    gather(2)


def sample_kernel(
    r_ref, w_ref, cell_ref, table_ref, sum_ref, v_ref, g_ref, grid_ref, hot_ref, tw_ref
):
    tw_ref[...] = twiddles(table_ref)
    upper = cell_ref[...] >> 8
    for block in range(16):
        place = lax.broadcasted_iota(jnp.int32, (16, WIDTH), 0) + block * 16
        hit = place == (cell_ref[...] & 255)
        hot_ref[block * 16 : block * 16 + 16, :] = jnp.where(hit, 1.0, 0.0).astype(BF16)

    def spread(m):
        for group in range(m * 3, m * 3 + 3):
            real, imag = unpacked(r_ref[pl.ds(group, 128, 12), :])
            v_ref[group * 128 : (group + 1) * 128, 0:128] = real.T
            v_ref[group * 128 : (group + 1) * 128, 128:256] = imag.T
        rows = slice(m * 384, (m + 1) * 384)
        v_high, v_low = halves(v_ref[rows, :])
        g_ref[rows, :] = (
            dot(v_high, table_ref[0:256, :])
            + dot(v_low, table_ref[0:256, :])
            + dot(v_high, table_ref[256:512, :])
        )
        one_row(2 * m)
        one_row(2 * m + 1)

    def one_row(row):
        for t in range(3):
            base = (((row // 2) * 3 + t) * 2 + row % 2) * 64
            values = []
            for k1 in range(8):
                rows = pl.ds(pl.multiple_of(base + k1 * 8, 8), 8)
                value = (g_ref[rows, 0:128], g_ref[rows, 128:256])
                if k1 > 0:
                    twiddle = (
                        tw_ref[0 + k1 * 8 : 8 + k1 * 8, :],
                        tw_ref[64 + k1 * 8 : 72 + k1 * 8, :],
                    )
                    value = cmul_conj(value, twiddle)
                values.append(value)
            values = dft8(values, 1.0)
            for n1 in range(8):
                start = (row * 4 + n1 // 2) * CHAN + t * 8
                lanes = slice((n1 % 2) * 128, (n1 % 2) * 128 + 128)
                grid_ref[pl.ds(pl.multiple_of(start, 8), 8), lanes] = values[n1][0]
                grid_ref[pl.ds(pl.multiple_of(start + HALF, 8), 8), lanes] = values[n1][1]

    def sample(m):
        rows = slice(m * 384, (m + 1) * 384)
        high, low = halves(grid_ref[rows, :])
        for chunk in range(8):
            lanes = slice(chunk * 256, (chunk + 1) * 256)
            picked = dot(high, hot_ref[:, lanes]) + dot(low, hot_ref[:, lanes])
            total = jnp.zeros((CHAN, 256), F32) if m == 0 else sum_ref[:, lanes]
            for part in range(8):
                hit = jnp.broadcast_to(upper[:, lanes] == m * 8 + part, (CHAN, 256))
                total = total + jnp.where(hit, picked[part * CHAN : (part + 1) * CHAN, :], 0.0)
            sum_ref[:, lanes] = total * w_ref[:, lanes] if m == 3 else total

    spread(0)
    for m in range(4):
        if m < 3:
            spread(m + 1)
        sample(m)


def finish_kernel(far_ref, near_ref, both_ref, side_ref, four_ref, out_ref, sum_ref):
    sum_ref[...] = far_ref[...] + near_ref[...]
    for cluster in range(4):
        lanes = slice(cluster * 4 * PIL, (cluster * 4 + 1) * PIL)
        sum_ref[:, lanes] += both_ref[:, cluster * PIL : (cluster + 1) * PIL].astype(F32)
        lanes = slice(cluster * PIL, (cluster + 1) * PIL)
        sum_ref[:, lanes] += both_ref[:, (cluster + 4) * PIL : (cluster + 5) * PIL].astype(F32)
    sum_ref[:, 3 * PIL : 4 * PIL] += side_ref[:, 4 * PIL : 5 * PIL].astype(F32)
    sum_ref[:, 15 * PIL : 16 * PIL] += four_ref[...].astype(F32)
    for slab in range(12):
        out_ref[slab] = sum_ref[slab * 4 : slab * 4 + 4, :]


def taylor(count, first):
    return [(-1.0) ** n / math.factorial(2 * n + first) for n in range(count)]


def horner(coefficients, square):
    total = jnp.full_like(square, coefficients[-1])
    for coefficient in coefficients[-2::-1]:
        total = total * square + coefficient
    return total


def near_kernel(
    list_ref, own_ref, both_ref, side_ref, four_ref, mix_ref,
    near_ref, back_one, back_side, back_four, all_ref, pos_ref, sum_ref,
):
    start = 0
    for data in (own_ref[...], both_ref[...], side_ref[:, 3 * PIL : 4 * PIL], four_ref[...]):
        width = data.shape[1]
        all_ref[:, start : start + width] = data[0:CHAN, :]
        pos_ref[:, start : start + width] = data[CHAN : CHAN + 16, :].astype(F32)
        start += width
    sum_ref[...] = jnp.zeros_like(sum_ref)
    wide_pos = list_ref[24]
    narrow_pos = list_ref[25]
    used = list_ref[26]
    local = lax.broadcasted_iota(jnp.int32, (1, PIL), 1)

    def place(wide, narrow, cluster, window):
        across = ((wide * CCX + cluster // CCY) * PCX + local // PCY).astype(F32)
        along = ((narrow * CCY + cluster % CCY) * PCY + local % PCY).astype(F32)
        return across * PITCH + pos_ref[0:1, window], along * PITCH + pos_ref[1:2, window]

    def column(vector):
        return jnp.broadcast_to(vector, (PIL, PIL)).T

    def mixed(values):
        return dot(mix_ref[...], values).astype(BF16)

    def one_slot(slot):
        direction = list_ref[slot * 3]
        own = list_ref[slot * 3 + 1]
        far = list_ref[slot * 3 + 2]
        move_wide = jnp.where(direction == 4, -1, jnp.where(direction >= 2, 1, 0))
        move_narrow = jnp.where(direction == 1, 1, jnp.where(direction >= 3, -1, 0))
        index = jnp.where(direction == 1, 16 + far // 4, far)
        index = jnp.where(direction == 2, 20 + far, index)
        index = jnp.where(direction == 3, 24, index)
        index = jnp.where(direction == 4, 25, index)
        own_window = pl.ds(pl.multiple_of(own * PIL, PIL), PIL)
        far_window = pl.ds(pl.multiple_of(index * PIL, PIL), PIL)
        own_x, own_y = place(wide_pos, narrow_pos, own, own_window)
        far_x, far_y = place(wide_pos + move_wide, narrow_pos + move_narrow, far, far_window)
        delta_x = column(own_x) - far_x
        delta_y = column(own_y) - far_y
        square = delta_x * delta_x + delta_y * delta_y
        over = lax.rsqrt(square)
        distance = square * over
        half_turns = (distance - jnp.round(distance)) * math.pi
        half_square = half_turns * half_turns
        half_sine = horner(taylor(7, 1), half_square) * half_turns
        half_cosine = horner(taylor(8, 0), half_square)
        cosine = 1.0 - 2.0 * half_sine * half_sine
        sine = 2.0 * half_sine * half_cosine
        unit_x = delta_x * over
        unit_y = delta_y * over
        inverse = over * (1.0 / (2.0 * math.pi))
        inverse_square = inverse * inverse
        green = (cosine * inverse, sine * inverse)
        term_a = cmul(green, (1.0 - inverse_square, inverse))
        term_b = cmul(green, (3.0 * inverse_square - 1.0, -3.0 * inverse))
        term_c = (green[0] - green[1] * inverse, green[1] + green[0] * inverse)
        unit_xx = unit_x * unit_x
        unit_xy = unit_x * unit_y
        unit_yy = unit_y * unit_y
        own_mixed = mixed(all_ref[:, own_window])
        far_mixed = mixed(all_ref[:, far_window])
        fields = []
        for field in range(6):
            for part in range(2):
                value = (
                    term_a[part],
                    term_b[part] * unit_xx,
                    term_b[part] * unit_xy,
                    term_b[part] * unit_yy,
                    term_c[part] * unit_x,
                    term_c[part] * unit_y,
                )[field].astype(BF16)
                fields.append(value)
        far_wide = jnp.concatenate([far_mixed[k * CHAN : (k + 1) * CHAN] for k in range(12)], axis=1)
        own_wide = jnp.concatenate([own_mixed[k * CHAN : (k + 1) * CHAN] for k in range(12)], axis=1)
        to_own = dot(far_wide, jnp.concatenate(fields, axis=1), 1, 1)
        to_far = dot(own_wide, jnp.concatenate(fields, axis=0), 1, 0)
        active = jnp.where(slot < used, 1.0, 0.0)
        return own_window, far_window, to_own * active, to_far * active

    def some_slots(step, carry):
        results = [one_slot(step * 4 + place) for place in range(4)]
        for own_window, far_window, to_own, to_far in results:
            sum_ref[:, own_window] += to_own
            sum_ref[:, far_window] += to_far
        return carry

    lax.fori_loop(0, (used + 3) // 4, some_slots, 0)
    near_ref[...] = sum_ref[:, 0:WIDTH]
    start = WIDTH
    for back in (back_one, back_side, back_four):
        width = back.shape[1]
        back[...] = sum_ref[:, start : start + width].astype(BF16)
        start += width


def shape(dims, kind=F32):
    return jax.ShapeDtypeStruct(dims, kind)


def shift(value, move_wide, move_narrow):
    pairs = []
    for wide in range(N_WIDE):
        for narrow in range(N_NARROW):
            to_wide, to_narrow = wide + move_wide, (narrow + move_narrow) % N_NARROW
            if 0 <= to_wide < N_WIDE:
                pairs.append((wide * N_NARROW + narrow, to_wide * N_NARROW + to_narrow))
    return lax.ppermute(value, AXES, pairs)


PARAMS = pltpu.CompilerParams(vmem_limit_bytes=48 * MIB)


def cost(flops, size):
    return pl.CostEstimate(flops=flops, bytes_accessed=size, transcendentals=0)


def pack_call(x, jitter):
    return pl.pallas_call(
        pack_kernel,
        out_shape=[
            shape((64, WIDTH), BF16),
            shape((64, 4 * PIL), BF16),
            shape((64, 4 * PIL), BF16),
            shape((64, PIL), BF16),
        ],
        scratch_shapes=[pltpu.VMEM((64, WIDTH), F32)],
        compiler_params=PARAMS,
        cost_estimate=cost(1_000_000, MIB // 2),
    )(x, jitter)


def rows_call(x, w, cell, table):
    return pl.pallas_call(
        rows_kernel,
        in_specs=[pl.BlockSpec(memory_space=pltpu.HBM)] * 4,
        out_shape=shape((DEVICES * 12, 128), jnp.int32),
        scratch_shapes=[
            pltpu.VMEM((12, 4, WIDTH), BF16),
            pltpu.VMEM((1, WIDTH), F32),
            pltpu.VMEM((1, WIDTH), jnp.int32),
            pltpu.VMEM((640, 256), BF16),
            pltpu.VMEM((CHAN, WIDTH), F32),
            pltpu.VMEM((CHAN, WIDTH), BF16),
            pltpu.VMEM((1536, WIDTH), BF16),
            pltpu.VMEM((2, 256, WIDTH), BF16),
            pltpu.VMEM((1536, 256), F32),
            pltpu.VMEM((1536, 256), F32),
            pltpu.VMEM((128, 128), F32),
            pltpu.SemaphoreType.DMA((4,)),
        ],
        compiler_params=pltpu.CompilerParams(vmem_limit_bytes=63 * MIB),
        cost_estimate=cost(3_800_000_000, 4 * MIB),
    )(x, w, cell, table)


def near_call(spots, own, both, side, four, mixing):
    return pl.pallas_call(
        near_kernel,
        in_specs=[pl.BlockSpec(memory_space=pltpu.SMEM)] + [pl.BlockSpec(memory_space=pltpu.VMEM)] * 5,
        out_shape=[
            shape((CHAN, WIDTH)),
            shape((CHAN, 4 * PIL), BF16),
            shape((CHAN, 5 * PIL), BF16),
            shape((CHAN, PIL), BF16),
        ],
        scratch_shapes=[
            pltpu.VMEM((CHAN, WIDTH + HALO * PIL), BF16),
            pltpu.VMEM((16, WIDTH + HALO * PIL), F32),
            pltpu.VMEM((CHAN, WIDTH + HALO * PIL), F32),
        ],
        compiler_params=PARAMS,
        cost_estimate=cost(8_000_000_000, 4 * MIB),
    )(spots, own, both, side, four, mixing)


def columns_call(columns, transfer, forward, backward, column_table, lane_table):
    return pl.pallas_call(
        columns_kernel,
        out_shape=shape((DEVICES * 12, 128), jnp.int32),
        scratch_shapes=[pltpu.VMEM((256, 1536), F32)] * 3,
        compiler_params=PARAMS,
        cost_estimate=cost(2_000_000_000, 6 * MIB),
    )(columns, transfer, forward, backward, column_table, lane_table)


def sample_call(rows, w, cell, table):
    return pl.pallas_call(
        sample_kernel,
        out_shape=shape((CHAN, WIDTH)),
        scratch_shapes=[
            pltpu.VMEM((1536, 256), F32),
            pltpu.VMEM((1536, 256), F32),
            pltpu.VMEM((1536, 256), F32),
            pltpu.VMEM((256, WIDTH), BF16),
            pltpu.VMEM((128, 128), F32),
        ],
        compiler_params=PARAMS,
        cost_estimate=cost(3_800_000_000, 4 * MIB),
    )(rows, w, cell, table)


def finish_call(far, near, both, side, four):
    return pl.pallas_call(
        finish_kernel,
        out_shape=shape((12, 4, WIDTH)),
        scratch_shapes=[pltpu.VMEM((CHAN, WIDTH), F32)],
        compiler_params=PARAMS,
        cost_estimate=cost(1_000_000, 2 * MIB),
    )(far, near, both, side, four)


def exchange(message):
    message = message.reshape(DEVICES * 3, 4, 128)
    message = lax.all_to_all(message, AXES, split_axis=0, concat_axis=0, tiled=True)
    return message.reshape(DEVICES * 12, 128)


def local(incident, jitter, weights, cells, pair_list, pair_count, kernel):
    x = incident.transpose(0, 2, 1, 3).reshape(12, ANG, WIDTH)
    w = weights.reshape(1, WIDTH)
    cell = cells.reshape(1, WIDTH)
    forward = jnp.asarray(dft_table(-1.0))
    table = jnp.asarray(row_table())

    message = rows_call(x, w, cell, table)
    columns = exchange(message)
    own, one, two, four = pack_call(x, jitter)
    side = shift(two, -1, 1)
    four = shift(four, 1, 1)
    both = shift(jnp.concatenate([one, side], axis=1), 0, -1)

    transfer = kernel.reshape(2, 2, 4, 128, 8).transpose(0, 2, 3, 1, 4)
    transfer = jnp.broadcast_to(transfer[..., None], (2, 4, 128, 2, 8, 8)).reshape(2, 512, 128)
    message = columns_call(
        columns,
        transfer,
        forward,
        jnp.asarray(dft_table(1.0, 1.0 / 1048576)),
        jnp.asarray(column_twiddle()),
        jnp.asarray(lane_twiddle()),
    )
    rows = exchange(message)

    spots = jnp.concatenate(
        [
            pair_list.reshape(PAIRS * 3),
            lax.axis_index("wide").reshape(1),
            lax.axis_index("narrow").reshape(1),
            pair_count,
        ]
    )
    near, one, side, four = near_call(spots, own, both, side, four, jnp.asarray(mixing_table()))
    side = shift(side, 1, -1)
    four = shift(four, -1, -1)
    both = shift(jnp.concatenate([one, side[:, 0 : 4 * PIL]], axis=1), 0, 1)
    far = sample_call(rows, w, cell, table)
    coupled = finish_call(far, near, both, side, four)
    return coupled.reshape(2, 6, ANG, WIDTH).transpose(0, 2, 1, 3)


def solution(mesh):
    in_specs = (
        P(None, None, None, AXES),
        P(None, AXES),
        P(AXES),
        P(AXES),
        P(AXES, None, None),
        P(AXES),
        P(None, None, AXES),
    )
    return jax.shard_map(
        local, mesh=mesh, in_specs=in_specs, out_specs=P(None, None, None, AXES), check_vma=False
    )
```

```python
import math

import jax
import jax.numpy as jnp
import numpy as np
from jax import lax
from jax.experimental import pallas as pl
from jax.experimental.pallas import tpu as pltpu
from jax.sharding import PartitionSpec as P

ANG = 4
PCX = 8
PCY = 16
CCX = 4
CCY = 4
PIL = 128
CHAN = 48
HALF = 24
WIDTH = 2048
PAIRS = 8
N_WIDE = 16
N_NARROW = 8
DEVICES = 128
AXES = ("wide", "narrow")
PITCH = 0.4
BF16 = jnp.bfloat16
F32 = jnp.float32
HALO = 10
MIB = 1 << 20


def split_table(table):
    high = table.astype(BF16)
    low = (table - high.astype(np.float64)).astype(BF16)
    return np.stack([high, low])


def dft_table(sign, scale=1.0):
    ids = np.arange(128)
    angles = (ids[:, None] * ids[None, :] % 128) * (2.0 * math.pi / 128)
    cosine = np.cos(angles) * scale
    sine = np.sin(angles) * scale * sign
    return split_table(np.block([[cosine, -sine], [sine, cosine]]))


def row_table():
    k1 = np.repeat(np.arange(8), 8)
    angles = (k1[:, None] * np.arange(128)[None, :]) * (2.0 * math.pi / 1024)
    twiddle = split_table(np.concatenate([np.cos(angles), -np.sin(angles)]))
    return np.concatenate([*dft_table(-1.0), np.concatenate([*twiddle], axis=1)])


def column_twiddle():
    row = (np.arange(128) // 64)[None, None, :] + 2 * np.arange(4)[:, None, None]
    angles = (row * np.arange(128)[None, :, None]) * (2.0 * math.pi / 1024)
    return np.stack([np.cos(angles), -np.sin(angles)]).reshape(2, 512, 128).astype(np.float32)


def lane_twiddle():
    side = (np.arange(128) // 64)[None, :]
    angles = np.arange(4)[:, None] * side * (2.0 * math.pi / 8)
    table = np.concatenate([np.cos(angles), -np.sin(angles), np.where(side == 0, 1.0, -1.0)])
    return np.concatenate([table, np.zeros((7, 128))]).astype(np.float32)


def mixing_table():
    table = np.zeros((6, 6, 6), np.float32)
    for member in range(6):
        table[0, member, member] = 1.0
    for offset in (0, 3):
        table[1, offset, offset] = 1.0
        table[2, offset, offset + 1] = 1.0
        table[2, offset + 1, offset] = 1.0
        table[3, offset + 1, offset + 1] = 1.0
    table[4, 2, 4] = 1.0
    table[4, 4, 2] = 1.0
    table[4, 1, 5] = -1.0
    table[4, 5, 1] = -1.0
    table[5, 0, 5] = 1.0
    table[5, 5, 0] = 1.0
    table[5, 2, 3] = -1.0
    table[5, 3, 2] = -1.0
    parts = np.zeros((2, 2, 2), np.float32)
    parts[0] = np.eye(2)
    parts[1] = np.array([[0.0, -1.0], [1.0, 0.0]])
    full = np.einsum("fab,rop,gh->froagpbh", table, parts, np.eye(ANG))
    return full.reshape(12 * CHAN, CHAN).astype(BF16)


def dot(left, right, left_dim=1, right_dim=0):
    return lax.dot_general(
        left, right, (((left_dim,), (right_dim,)), ((), ())), preferred_element_type=F32
    )


def halves(value):
    high = value.astype(BF16)
    return high, (value - high.astype(F32)).astype(BF16)


STEP = 585.0
FLOOR = 36.0


def coded(value):
    size = jnp.log(jnp.maximum(jnp.abs(value), 2.0**-FLOOR))
    code = size * (STEP / math.log(2.0)) + (FLOOR * STEP + 0.5)
    return (code * jnp.clip(value * 2.0**60, -1.0, 1.0)).astype(jnp.int32)


def decoded(code):
    code = code.astype(F32)
    return jnp.exp2(jnp.abs(code) * (1.0 / STEP) - FLOOR) * jnp.clip(code, -1.0, 1.0)


def packed(real, imag):
    return (coded(real) << 16) | (coded(imag) & 0xFFFF)


def unpacked(word):
    return decoded(word >> 16), decoded((word << 16) >> 16)


def cadd(left, right):
    return (left[0] + right[0], left[1] + right[1])


def csub(left, right):
    return (left[0] - right[0], left[1] - right[1])


def cmul(left, right):
    return (left[0] * right[0] - left[1] * right[1], left[0] * right[1] + left[1] * right[0])


def cmul_conj(left, right):
    return (left[0] * right[0] + left[1] * right[1], left[1] * right[0] - left[0] * right[1])


def turn(value, sign):
    if sign < 0:
        return (value[1], -value[0])
    return (-value[1], value[0])


def dft4(values, sign):
    even, odd = cadd(values[0], values[2]), csub(values[0], values[2])
    left, right = cadd(values[1], values[3]), turn(csub(values[1], values[3]), sign)
    return [cadd(even, left), cadd(odd, right), csub(even, left), csub(odd, right)]


def dft8(values, sign):
    even = dft4(values[0::2], sign)
    odd = dft4(values[1::2], sign)
    root = math.sqrt(0.5)
    first, third = odd[1], odd[3]
    odd[1] = ((first[0] - sign * first[1]) * root, (first[1] + sign * first[0]) * root)
    odd[2] = turn(odd[2], sign)
    odd[3] = ((-third[0] - sign * third[1]) * root, (-third[1] + sign * third[0]) * root)
    return [cadd(e, o) for e, o in zip(even, odd)] + [csub(e, o) for e, o in zip(even, odd)]


def pack_kernel(x_ref, jitter_ref, own_ref, one_ref, two_ref, four_ref, pack_ref):
    for slab in range(12):
        pack_ref[slab * 4 : slab * 4 + 4, :] = x_ref[slab].astype(F32)
    pack_ref[CHAN : CHAN + 16, :] = jnp.zeros((16, WIDTH), F32)
    pack_ref[CHAN : CHAN + 2, :] = jitter_ref[...].astype(F32)
    own_ref[...] = pack_ref[...].astype(BF16)
    for cluster in range(4):
        one_ref[:, cluster * PIL : (cluster + 1) * PIL] = own_ref[:, cluster * 4 * PIL : (cluster * 4 + 1) * PIL]
    two_ref[...] = own_ref[:, 0 : 4 * PIL]
    four_ref[...] = own_ref[:, 15 * PIL : 16 * PIL]


def twiddles(table_ref):
    return table_ref[512:640, 0:128].astype(F32) + table_ref[512:640, 128:256].astype(F32)


def rows_kernel(
    x_hbm, w_hbm, cell_hbm, table_hbm, out_ref,
    x_ref, w_ref, cell_ref, table_ref, pack_ref, xb_ref, xt_ref, hot_ref, g_ref, b_ref, tw_ref, sems,
):
    pairs = ((cell_hbm, cell_ref), (w_hbm, w_ref), (x_hbm, x_ref), (table_hbm, table_ref))
    copies = [
        pltpu.make_async_copy(source, target, sems.at[place])
        for place, (source, target) in enumerate(pairs)
    ]
    for copy in copies:
        copy.start()
    copies[0].wait()
    copies[1].wait()
    cells = cell_ref[...]
    upper = cells >> 8
    weight = w_ref[...]
    high = weight.astype(BF16).astype(F32)
    low = weight - high
    for block in range(16):
        place = lax.broadcasted_iota(jnp.int32, (16, WIDTH), 0) + block * 16
        hit = place == (cells & 255)
        hot_ref[0, block * 16 : block * 16 + 16, :] = jnp.where(hit, high, 0.0).astype(BF16)
        hot_ref[1, block * 16 : block * 16 + 16, :] = jnp.where(hit, low, 0.0).astype(BF16)
    copies[2].wait()
    for slab in range(12):
        pack_ref[slab * 4 : slab * 4 + 4, :] = x_ref[slab].astype(F32)
    xb_ref[...] = pack_ref[...].astype(BF16)
    for part in range(32):
        mask = jnp.where(upper == part, 1.0, 0.0).astype(BF16)
        xt_ref[part * CHAN : (part + 1) * CHAN, :] = xb_ref[...] * mask
    for chunk in range(2):
        rows = slice(chunk * 768, (chunk + 1) * 768)
        piece = xt_ref[rows, :]
        g_ref[rows, :] = dot(piece, hot_ref[0], 1, 1) + dot(piece, hot_ref[1], 1, 1)

    copies[3].wait()
    tw_ref[...] = twiddles(table_ref)

    def one_row(row):
        for t in range(3):
            values = []
            for n1 in range(8):
                start = (row * 4 + n1 // 2) * CHAN + t * 8
                lanes = slice((n1 % 2) * 128, (n1 % 2) * 128 + 128)
                values.append(
                    (
                        g_ref[pl.ds(pl.multiple_of(start, 8), 8), lanes],
                        g_ref[pl.ds(pl.multiple_of(start + HALF, 8), 8), lanes],
                    )
                )
            values = dft8(values, -1.0)
            base = (((row // 2) * 3 + t) * 2 + row % 2) * 64
            for k1 in range(8):
                value = values[k1]
                if k1 > 0:
                    twiddle = (
                        tw_ref[0 + k1 * 8 : 8 + k1 * 8, :],
                        tw_ref[64 + k1 * 8 : 72 + k1 * 8, :],
                    )
                    value = cmul(value, twiddle)
                rows = pl.ds(pl.multiple_of(base + k1 * 8, 8), 8)
                b_ref[rows, 0:128] = value[0]
                b_ref[rows, 128:256] = value[1]

    for row in range(8):
        one_row(row)
    for pair in range(6):
        b_high, b_low = halves(b_ref[pair * 256 : (pair + 1) * 256, :])
        result = (
            dot(table_ref[0:256, :], b_high, 1, 1)
            + dot(table_ref[0:256, :], b_low, 1, 1)
            + dot(table_ref[256:512, :], b_high, 1, 1)
        )
        for side in range(2):
            lanes = slice(side * 128, (side + 1) * 128)
            out_ref[pl.ds(pair * 2 + side, 128, 12), :] = packed(result[0:128, lanes], result[128:256, lanes])


def columns_kernel(r_ref, kern_ref, fwd_ref, inv_ref, tw_ref, lane_ref, out_ref, v_ref, u_ref, y_ref):
    sign = lane_ref[8:9, :]

    def swap(value):
        return tuple(part * sign + pltpu.roll(part, 64, 1) for part in value)

    def lanes_of(t, m):
        return slice((t * 4 + m) * 128, (t * 4 + m + 1) * 128)

    def spread(t):
        for m in range(4):
            real, imag = unpacked(r_ref[pl.ds(m * 3 + t, 128, 12), :])
            v_ref[0:128, lanes_of(t, m)] = real
            v_ref[128:256, lanes_of(t, m)] = imag
        for chunk in range(2):
            lanes = slice((t * 2 + chunk) * 256, (t * 2 + chunk + 1) * 256)
            v_high, v_low = halves(v_ref[:, lanes])
            u_ref[:, lanes] = dot(fwd_ref[0], v_high) + dot(fwd_ref[0], v_low) + dot(fwd_ref[1], v_high)

    def multiply(t):
        for block in range(16):
            re_rows = slice(block * 8, block * 8 + 8)
            im_rows = slice(block * 8 + 128, block * 8 + 136)
            values, twiddles = [], []
            for m in range(4):
                rows = slice(m * 128 + block * 8, m * 128 + block * 8 + 8)
                twiddles.append((tw_ref[0, rows, :], tw_ref[1, rows, :]))
                lanes = lanes_of(t, m)
                values.append(cmul((u_ref[re_rows, lanes], u_ref[im_rows, lanes]), twiddles[m]))
            values = dft4(values, -1.0)
            for a in range(4):
                rows = slice(a * 128 + block * 8, a * 128 + block * 8 + 8)
                side = (lane_ref[a : a + 1, :], lane_ref[4 + a : 5 + a, :])
                value = values[a] if a == 0 else cmul(values[a], side)
                value = swap(cmul(swap(value), (kern_ref[0, rows, :], kern_ref[1, rows, :])))
                values[a] = value if a == 0 else cmul_conj(value, side)
            values = dft4(values, 1.0)
            for m in range(4):
                value = cmul_conj(values[m], twiddles[m])
                y_ref[re_rows, lanes_of(t, m)] = value[0]
                y_ref[im_rows, lanes_of(t, m)] = value[1]

    def gather(t):
        for chunk in range(2):
            lanes = slice((t * 2 + chunk) * 256, (t * 2 + chunk + 1) * 256)
            y_high, y_low = halves(y_ref[:, lanes])
            result = dot(inv_ref[0], y_high) + dot(inv_ref[0], y_low) + dot(inv_ref[1], y_high)
            for side in range(2):
                lanes = slice(side * 128, (side + 1) * 128)
                out_ref[pl.ds((chunk * 2 + side) * 3 + t, 128, 12), :] = packed(
                    result[0:128, lanes], result[128:256, lanes]
                )

    spread(0)
    spread(1)
    multiply(0)
    spread(2)
    gather(0)
    multiply(1)
    gather(1)
    multiply(2)
    gather(2)


def place_kernel(cell_ref, hot_ref):
    for block in range(16):
        place = lax.broadcasted_iota(jnp.int32, (16, WIDTH), 0) + block * 16
        hit = place == (cell_ref[...] & 255)
        hot_ref[block * 16 : block * 16 + 16, :] = jnp.where(hit, 1.0, 0.0).astype(BF16)


def sample_kernel(
    r_ref, w_ref, cell_ref, table_ref, hot_ref, sum_ref, v_ref, g_ref, grid_ref, tw_ref
):
    tw_ref[...] = twiddles(table_ref)
    upper = cell_ref[...] >> 8
    def spread(m):
        for group in range(m * 3, m * 3 + 3):
            real, imag = unpacked(r_ref[pl.ds(group, 128, 12), :])
            v_ref[group * 128 : (group + 1) * 128, 0:128] = real.T
            v_ref[group * 128 : (group + 1) * 128, 128:256] = imag.T
        rows = slice(m * 384, (m + 1) * 384)
        v_high, v_low = halves(v_ref[rows, :])
        g_ref[rows, :] = (
            dot(v_high, table_ref[0:256, :])
            + dot(v_low, table_ref[0:256, :])
            + dot(v_high, table_ref[256:512, :])
        )
        one_row(2 * m)
        one_row(2 * m + 1)

    def one_row(row):
        for t in range(3):
            base = (((row // 2) * 3 + t) * 2 + row % 2) * 64
            values = []
            for k1 in range(8):
                rows = pl.ds(pl.multiple_of(base + k1 * 8, 8), 8)
                value = (g_ref[rows, 0:128], g_ref[rows, 128:256])
                if k1 > 0:
                    twiddle = (
                        tw_ref[0 + k1 * 8 : 8 + k1 * 8, :],
                        tw_ref[64 + k1 * 8 : 72 + k1 * 8, :],
                    )
                    value = cmul_conj(value, twiddle)
                values.append(value)
            values = dft8(values, 1.0)
            for n1 in range(8):
                start = (row * 4 + n1 // 2) * CHAN + t * 8
                lanes = slice((n1 % 2) * 128, (n1 % 2) * 128 + 128)
                grid_ref[pl.ds(pl.multiple_of(start, 8), 8), lanes] = values[n1][0]
                grid_ref[pl.ds(pl.multiple_of(start + HALF, 8), 8), lanes] = values[n1][1]

    def sample(m):
        rows = slice(m * 384, (m + 1) * 384)
        high, low = halves(grid_ref[rows, :])
        for chunk in range(8):
            lanes = slice(chunk * 256, (chunk + 1) * 256)
            picked = dot(high, hot_ref[:, lanes]) + dot(low, hot_ref[:, lanes])
            total = jnp.zeros((CHAN, 256), F32) if m == 0 else sum_ref[:, lanes]
            for part in range(8):
                hit = jnp.broadcast_to(upper[:, lanes] == m * 8 + part, (CHAN, 256))
                total = total + jnp.where(hit, picked[part * CHAN : (part + 1) * CHAN, :], 0.0)
            sum_ref[:, lanes] = total * w_ref[:, lanes] if m == 3 else total

    spread(0)
    for m in range(4):
        if m < 3:
            spread(m + 1)
        sample(m)


def finish_kernel(far_ref, near_ref, both_ref, side_ref, four_ref, out_ref, sum_ref):
    sum_ref[...] = far_ref[...] + near_ref[...]
    for cluster in range(4):
        lanes = slice(cluster * 4 * PIL, (cluster * 4 + 1) * PIL)
        sum_ref[:, lanes] += both_ref[:, cluster * PIL : (cluster + 1) * PIL].astype(F32)
        lanes = slice(cluster * PIL, (cluster + 1) * PIL)
        sum_ref[:, lanes] += both_ref[:, (cluster + 4) * PIL : (cluster + 5) * PIL].astype(F32)
    sum_ref[:, 3 * PIL : 4 * PIL] += side_ref[:, 4 * PIL : 5 * PIL].astype(F32)
    sum_ref[:, 15 * PIL : 16 * PIL] += four_ref[...].astype(F32)
    for slab in range(12):
        out_ref[slab] = sum_ref[slab * 4 : slab * 4 + 4, :]


def taylor(count, first):
    return [(-1.0) ** n / math.factorial(2 * n + first) for n in range(count)]


def horner(coefficients, square):
    total = jnp.full_like(square, coefficients[-1])
    for coefficient in coefficients[-2::-1]:
        total = total * square + coefficient
    return total


def near_kernel(
    list_ref, own_ref, both_ref, side_ref, four_ref, mix_ref,
    near_ref, back_one, back_side, back_four, all_ref, pos_ref, sum_ref,
):
    start = 0
    for data in (own_ref[...], both_ref[...], side_ref[:, 3 * PIL : 4 * PIL], four_ref[...]):
        width = data.shape[1]
        all_ref[:, start : start + width] = data[0:CHAN, :]
        pos_ref[:, start : start + width] = data[CHAN : CHAN + 16, :].astype(F32)
        start += width
    sum_ref[...] = jnp.zeros_like(sum_ref)
    wide_pos = list_ref[24]
    narrow_pos = list_ref[25]
    used = list_ref[26]
    local = lax.broadcasted_iota(jnp.int32, (1, PIL), 1)

    def place(wide, narrow, cluster, window):
        across = ((wide * CCX + cluster // CCY) * PCX + local // PCY).astype(F32)
        along = ((narrow * CCY + cluster % CCY) * PCY + local % PCY).astype(F32)
        return across * PITCH + pos_ref[0:1, window], along * PITCH + pos_ref[1:2, window]

    def column(vector):
        return jnp.broadcast_to(vector, (PIL, PIL)).T

    def mixed(values):
        return dot(mix_ref[...], values).astype(BF16)

    def one_slot(slot):
        direction = list_ref[slot * 3]
        own = list_ref[slot * 3 + 1]
        far = list_ref[slot * 3 + 2]
        move_wide = jnp.where(direction == 4, -1, jnp.where(direction >= 2, 1, 0))
        move_narrow = jnp.where(direction == 1, 1, jnp.where(direction >= 3, -1, 0))
        index = jnp.where(direction == 1, 16 + far // 4, far)
        index = jnp.where(direction == 2, 20 + far, index)
        index = jnp.where(direction == 3, 24, index)
        index = jnp.where(direction == 4, 25, index)
        own_window = pl.ds(pl.multiple_of(own * PIL, PIL), PIL)
        far_window = pl.ds(pl.multiple_of(index * PIL, PIL), PIL)
        own_x, own_y = place(wide_pos, narrow_pos, own, own_window)
        far_x, far_y = place(wide_pos + move_wide, narrow_pos + move_narrow, far, far_window)
        delta_x = column(own_x) - far_x
        delta_y = column(own_y) - far_y
        square = delta_x * delta_x + delta_y * delta_y
        over = lax.rsqrt(square)
        distance = square * over
        half_turns = (distance - jnp.round(distance)) * math.pi
        half_square = half_turns * half_turns
        half_sine = horner(taylor(7, 1), half_square) * half_turns
        half_cosine = horner(taylor(8, 0), half_square)
        cosine = 1.0 - 2.0 * half_sine * half_sine
        sine = 2.0 * half_sine * half_cosine
        unit_x = delta_x * over
        unit_y = delta_y * over
        inverse = over * (1.0 / (2.0 * math.pi))
        inverse_square = inverse * inverse
        green = (cosine * inverse, sine * inverse)
        term_a = cmul(green, (1.0 - inverse_square, inverse))
        term_b = cmul(green, (3.0 * inverse_square - 1.0, -3.0 * inverse))
        term_c = (green[0] - green[1] * inverse, green[1] + green[0] * inverse)
        unit_xx = unit_x * unit_x
        unit_xy = unit_x * unit_y
        unit_yy = unit_y * unit_y
        own_mixed = mixed(all_ref[:, own_window])
        far_mixed = mixed(all_ref[:, far_window])
        fields = []
        for field in range(6):
            for part in range(2):
                value = (
                    term_a[part],
                    term_b[part] * unit_xx,
                    term_b[part] * unit_xy,
                    term_b[part] * unit_yy,
                    term_c[part] * unit_x,
                    term_c[part] * unit_y,
                )[field].astype(BF16)
                fields.append(value)
        far_wide = jnp.concatenate([far_mixed[k * CHAN : (k + 1) * CHAN] for k in range(12)], axis=1)
        own_wide = jnp.concatenate([own_mixed[k * CHAN : (k + 1) * CHAN] for k in range(12)], axis=1)
        to_own = dot(far_wide, jnp.concatenate(fields, axis=1), 1, 1)
        to_far = dot(own_wide, jnp.concatenate(fields, axis=0), 1, 0)
        active = jnp.where(slot < used, 1.0, 0.0)
        return own_window, far_window, to_own * active, to_far * active

    def some_slots(step, carry):
        results = [one_slot(step * 4 + place) for place in range(4)]
        for own_window, far_window, to_own, to_far in results:
            sum_ref[:, own_window] += to_own
            sum_ref[:, far_window] += to_far
        return carry

    lax.fori_loop(0, (used + 3) // 4, some_slots, 0)
    near_ref[...] = sum_ref[:, 0:WIDTH]
    start = WIDTH
    for back in (back_one, back_side, back_four):
        width = back.shape[1]
        back[...] = sum_ref[:, start : start + width].astype(BF16)
        start += width


def shape(dims, kind=F32):
    return jax.ShapeDtypeStruct(dims, kind)


def shift(value, move_wide, move_narrow):
    pairs = []
    for wide in range(N_WIDE):
        for narrow in range(N_NARROW):
            to_wide, to_narrow = wide + move_wide, (narrow + move_narrow) % N_NARROW
            if 0 <= to_wide < N_WIDE:
                pairs.append((wide * N_NARROW + narrow, to_wide * N_NARROW + to_narrow))
    return lax.ppermute(value, AXES, pairs)


PARAMS = pltpu.CompilerParams(vmem_limit_bytes=48 * MIB)


def cost(flops, size):
    return pl.CostEstimate(flops=flops, bytes_accessed=size, transcendentals=0)


def pack_call(x, jitter):
    return pl.pallas_call(
        pack_kernel,
        out_shape=[
            shape((64, WIDTH), BF16),
            shape((64, 4 * PIL), BF16),
            shape((64, 4 * PIL), BF16),
            shape((64, PIL), BF16),
        ],
        scratch_shapes=[pltpu.VMEM((64, WIDTH), F32)],
        compiler_params=PARAMS,
        cost_estimate=cost(1_000_000, MIB // 2),
    )(x, jitter)


def rows_call(x, w, cell, table):
    return pl.pallas_call(
        rows_kernel,
        in_specs=[pl.BlockSpec(memory_space=pltpu.HBM)] * 4,
        out_shape=shape((DEVICES * 12, 128), jnp.int32),
        scratch_shapes=[
            pltpu.VMEM((12, 4, WIDTH), BF16),
            pltpu.VMEM((1, WIDTH), F32),
            pltpu.VMEM((1, WIDTH), jnp.int32),
            pltpu.VMEM((640, 256), BF16),
            pltpu.VMEM((CHAN, WIDTH), F32),
            pltpu.VMEM((CHAN, WIDTH), BF16),
            pltpu.VMEM((1536, WIDTH), BF16),
            pltpu.VMEM((2, 256, WIDTH), BF16),
            pltpu.VMEM((1536, 256), F32),
            pltpu.VMEM((1536, 256), F32),
            pltpu.VMEM((128, 128), F32),
            pltpu.SemaphoreType.DMA((4,)),
        ],
        compiler_params=pltpu.CompilerParams(vmem_limit_bytes=63 * MIB),
        cost_estimate=cost(3_800_000_000, 4 * MIB),
    )(x, w, cell, table)


def near_call(spots, own, both, side, four, mixing):
    return pl.pallas_call(
        near_kernel,
        in_specs=[pl.BlockSpec(memory_space=pltpu.SMEM)] + [pl.BlockSpec(memory_space=pltpu.VMEM)] * 5,
        out_shape=[
            shape((CHAN, WIDTH)),
            shape((CHAN, 4 * PIL), BF16),
            shape((CHAN, 5 * PIL), BF16),
            shape((CHAN, PIL), BF16),
        ],
        scratch_shapes=[
            pltpu.VMEM((CHAN, WIDTH + HALO * PIL), BF16),
            pltpu.VMEM((16, WIDTH + HALO * PIL), F32),
            pltpu.VMEM((CHAN, WIDTH + HALO * PIL), F32),
        ],
        compiler_params=PARAMS,
        cost_estimate=cost(8_000_000_000, 4 * MIB),
    )(spots, own, both, side, four, mixing)


def columns_call(columns, transfer, forward, backward, column_table, lane_table):
    return pl.pallas_call(
        columns_kernel,
        out_shape=shape((DEVICES * 12, 128), jnp.int32),
        scratch_shapes=[pltpu.VMEM((256, 1536), F32)] * 3,
        compiler_params=PARAMS,
        cost_estimate=cost(2_000_000_000, 6 * MIB),
    )(columns, transfer, forward, backward, column_table, lane_table)


def place_call(cell):
    return pl.pallas_call(
        place_kernel,
        out_shape=shape((256, WIDTH), BF16),
        compiler_params=PARAMS,
        cost_estimate=cost(500_000_000, MIB),
    )(cell)


def sample_call(rows, w, cell, table, hot):
    return pl.pallas_call(
        sample_kernel,
        out_shape=shape((CHAN, WIDTH)),
        scratch_shapes=[
            pltpu.VMEM((1536, 256), F32),
            pltpu.VMEM((1536, 256), F32),
            pltpu.VMEM((1536, 256), F32),
            pltpu.VMEM((128, 128), F32),
        ],
        compiler_params=PARAMS,
        cost_estimate=cost(3_800_000_000, 4 * MIB),
    )(rows, w, cell, table, hot)


def finish_call(far, near, both, side, four):
    return pl.pallas_call(
        finish_kernel,
        out_shape=shape((12, 4, WIDTH)),
        scratch_shapes=[pltpu.VMEM((CHAN, WIDTH), F32)],
        compiler_params=PARAMS,
        cost_estimate=cost(1_000_000, 2 * MIB),
    )(far, near, both, side, four)


def exchange(message):
    message = message.reshape(DEVICES * 3, 4, 128)
    message = lax.all_to_all(message, AXES, split_axis=0, concat_axis=0, tiled=True)
    return message.reshape(DEVICES * 12, 128)


def local(incident, jitter, weights, cells, pair_list, pair_count, kernel):
    x = incident.transpose(0, 2, 1, 3).reshape(12, ANG, WIDTH)
    w = weights.reshape(1, WIDTH)
    cell = cells.reshape(1, WIDTH)
    forward = jnp.asarray(dft_table(-1.0))
    table = jnp.asarray(row_table())

    message = rows_call(x, w, cell, table)
    columns = exchange(message)
    own, one, two, four = pack_call(x, jitter)
    side = shift(two, -1, 1)
    four = shift(four, 1, 1)
    both = shift(jnp.concatenate([one, side], axis=1), 0, -1)

    transfer = kernel.reshape(2, 2, 4, 128, 8).transpose(0, 2, 3, 1, 4)
    transfer = jnp.broadcast_to(transfer[..., None], (2, 4, 128, 2, 8, 8)).reshape(2, 512, 128)
    message = columns_call(
        columns,
        transfer,
        forward,
        jnp.asarray(dft_table(1.0, 1.0 / 1048576)),
        jnp.asarray(column_twiddle()),
        jnp.asarray(lane_twiddle()),
    )
    rows = exchange(message)

    spots = jnp.concatenate(
        [
            pair_list.reshape(PAIRS * 3),
            lax.axis_index("wide").reshape(1),
            lax.axis_index("narrow").reshape(1),
            pair_count,
        ]
    )
    near, one, side, four = near_call(spots, own, both, side, four, jnp.asarray(mixing_table()))
    side = shift(side, 1, -1)
    four = shift(four, -1, -1)
    both = shift(jnp.concatenate([one, side[:, 0 : 4 * PIL]], axis=1), 0, 1)
    far = sample_call(rows, w, cell, table, place_call(cell))
    coupled = finish_call(far, near, both, side, four)
    return coupled.reshape(2, 6, ANG, WIDTH).transpose(0, 2, 1, 3)


def solution(mesh):
    in_specs = (
        P(None, None, None, AXES),
        P(None, AXES),
        P(AXES),
        P(AXES),
        P(AXES, None, None),
        P(AXES),
        P(None, None, AXES),
    )
    return jax.shard_map(
        local, mesh=mesh, in_specs=in_specs, out_specs=P(None, None, None, AXES), check_vma=False
    )
```
